32 devices in a mesh: row: 4 (over z), col: 8 (over y, x, core).
Axes of the slice: x: 2, y: 2, z: 4, core: 2. Of those that a mesh axis runs over, the one named last changes fastest.
Arguments:
- descriptors: bfloat16 [8192, 128], P('row'), may hold values from -6 to 6
- image_counts: int32 [32], replicated, may hold values from 64 to 256
- pair_list: int32 [256, 2], P(('row', 'col')), may hold values from 0 to 31, as said below
- warm_start: bfloat16 [8192, 8192], P('row', 'col'), may hold values from 0 to 1
- factor_init: float32 [8192, 256], P('col'), may hold values from -0.3 to 0.3
Outputs:
- assignment: bfloat16 [8192, 8192], P('row', 'col')
- dual_var: float32 [8192, 8192], P('row', 'col')
The draws below stay inside these ranges and needn't reach their ends.
Inputs may be any that keep to these rules, and one draw needn't show every extreme that they name: `pair_list`: pairs are distinct. The 8 pairs on each device have their first image in that device's row block of 8 images, and at most 2 of them have their second image in any one column block of 4 images; in every row block some column block receives exactly 2 pairs from every device of that row group.
All inputs are finite; a program needn't handle non-finite values.
Results may differ from the reference program's by a relative error of at most 0.00055.
The reference program's roundings to bfloat16 on the way (of `unit`) count: a program that leaves them out, or rounds other values in their place, can miss the bound.
Values may be sent and summed in bfloat16 or wider, within the bound.
A program may use at most 128 MiB of HBM per device.

```python
import jax
import jax.numpy as jnp
from jax import lax

KP = 256
DESC = 128
RANK = 256
IMG_ROW = 8
ITERS = 2
CAP = 2
IMAGES = 32
IMG_COL = 4
KEYPOINTS = 8192
PAIR_DEV = 8
N_ROW = 4
N_COL = 8


def draw_pair_list(key, part):
    key_star, key_dest, key_place, key_order = jax.random.split(key, 4)
    cells = IMG_ROW * IMG_COL
    full_dest = jax.random.randint(key_star, (N_ROW,), 0, N_COL)
    dest_keys = jax.random.split(key_dest, N_ROW * N_COL)
    others = jax.vmap(lambda one_key: jax.random.permutation(one_key, N_COL - 1))(dest_keys).reshape(N_ROW, N_COL, N_COL - 1)
    dest_iota = jnp.arange(N_COL, dtype=jnp.int32)
    other_index = dest_iota[None, :] - (dest_iota[None, :] > full_dest[:, None]).astype(jnp.int32)
    other_index = jnp.minimum(other_index, N_COL - 2)
    index_full = jnp.broadcast_to(other_index[:, None, :], (N_ROW, N_COL, N_COL))
    ranks = jnp.take_along_axis(others, index_full, axis=2)
    quarter = N_COL // 4
    counts = jnp.where(ranks < quarter, 2, jnp.where(ranks < 2 * quarter + 1, 0, 1))
    counts = jnp.where(dest_iota[None, None, :] == full_dest[:, None, None], 2, counts).astype(jnp.int32)
    offsets = jnp.cumsum(counts, axis=1) - counts
    place_keys = jax.random.split(key_place, N_ROW * N_COL)
    positions = jax.vmap(lambda one_key: jax.random.permutation(one_key, cells))(place_keys).reshape(N_ROW, N_COL, cells)
    cap_iota = jnp.arange(CAP, dtype=jnp.int32)
    wanted = offsets[:, :, :, None] + cap_iota[None, None, None, :]
    used = cap_iota[None, None, None, :] < counts[:, :, :, None]
    wanted = jnp.minimum(wanted, cells - 1)
    wanted_flat = wanted.reshape(N_ROW, N_COL, N_COL * CAP)
    spread = jnp.broadcast_to(positions[:, None, :, :], (N_ROW, N_COL, N_COL, cells))
    spread = jnp.repeat(spread, CAP, axis=2)
    picked = jnp.take_along_axis(spread, wanted_flat[:, :, :, None], axis=3)[:, :, :, 0]
    row_iota = jnp.arange(N_ROW, dtype=jnp.int32)
    dest_slots = jnp.repeat(dest_iota, CAP)
    first_image = row_iota[:, None, None] * IMG_ROW + picked // IMG_COL
    second_image = dest_slots[None, None, :] * IMG_COL + picked % IMG_COL
    used_flat = used.reshape(N_ROW, N_COL, N_COL * CAP).astype(jnp.int32)
    slot_iota = jnp.arange(N_COL * CAP, dtype=jnp.int32)
    sort_score = (1 - used_flat) * (N_COL * CAP) + slot_iota[None, None, :]
    order = jnp.argsort(sort_score, axis=2)[:, :, :PAIR_DEV]
    first_kept = jnp.take_along_axis(first_image, order, axis=2)
    second_kept = jnp.take_along_axis(second_image, order, axis=2)
    order_keys = jax.random.split(key_order, N_ROW * N_COL)
    shuffle = jax.vmap(lambda one_key: jax.random.permutation(one_key, PAIR_DEV))(order_keys).reshape(N_ROW, N_COL, PAIR_DEV)
    first_kept = jnp.take_along_axis(first_kept, shuffle, axis=2)
    second_kept = jnp.take_along_axis(second_kept, shuffle, axis=2)
    stacked = jnp.stack([first_kept, second_kept], axis=3)
    return stacked.reshape(N_ROW * N_COL * PAIR_DEV, 2).astype(jnp.int32)


def place_ends(drawn, stream_key, least, top_value):
    longest = drawn.shape.index(max(drawn.shape))
    spots = []
    for shift in (0, 1):
        where = [jax.random.randint(jax.random.fold_in(stream_key, axis), (), 0, length) for axis, length in enumerate(drawn.shape)]
        where[longest] = (where[longest] + shift) % drawn.shape[longest]
        spots.append(tuple(where))
    return drawn.at[spots[0]].set(least).at[spots[1]].set(top_value)


def levels(own_key, extent, cuts, least, high):
    loudness = 1.0
    for position, parts in cuts:
        draws = jax.random.uniform(jax.random.fold_in(jax.random.fold_in(own_key, 6), position), (parts,), jnp.float32, least / len(cuts), high / len(cuts))
        loudness = loudness * jnp.repeat(jnp.exp(draws), extent[position] // parts).reshape((-1,) + (1,) * (len(extent) - 1 - position))
    return loudness


def normal_values(stream_key, extent, scale, limit, pieces=(), kind=jnp.bfloat16):
    entries = jax.random.normal(stream_key, extent, jnp.float32) * scale
    if len(pieces) > 0:
        entries = levels(stream_key, extent, pieces, -0.22, 0.18) * entries
    return jnp.clip(entries, min=-limit, max=limit).astype(kind)


def setup_inputs(seed: int = 0) -> dict:
    seeds = jax.random.split(jax.random.key(seed), 6)
    return {
        "descriptors": normal_values(seeds[0], (KEYPOINTS, DESC), 1.0, 6.0, ((0, 4),)),
        "image_counts": place_ends(jax.random.randint(seeds[1], (IMAGES,), KP // 4, KP + 1), jax.random.fold_in(seeds[1], 1), KP // 4, KP).astype(jnp.int32),
        "pair_list": draw_pair_list(jax.random.fold_in(seeds[5], 71), 0),
        "warm_start": jnp.clip(1.0 * jax.random.uniform(seeds[3], (KEYPOINTS, KEYPOINTS), jnp.float32) ** levels(seeds[3], (KEYPOINTS, KEYPOINTS), ((0, 4), (1, 8)), -0.2, 0.2), 0.0, 1.0).astype(jnp.bfloat16),
        "factor_init": normal_values(seeds[4], (KEYPOINTS, RANK), 0.05, 0.3, ((0, 8),), jnp.float32),
    }


EPSILON = 1e-06
SHARPNESS = 10.0
PENALTY = 2.0
RIDGE = 16.0
EXACT = lax.Precision.HIGHEST

def ridge_apply(partial_sum, gram_matrix):
    factor_low = jnp.linalg.cholesky(gram_matrix)
    half_solve = lax.linalg.triangular_solve(factor_low, partial_sum, left_side=False, lower=True, transpose_a=True)
    return lax.linalg.triangular_solve(factor_low, half_solve, left_side=False, lower=True, transpose_a=False)

def reference(descriptors, image_counts, pair_list, warm_start, factor_init):
    wide = descriptors.astype(jnp.float32)
    unit = (wide * lax.rsqrt(DESC * (lax.optimization_barrier(jnp.mean(wide * wide, axis=1, keepdims=True)) + EPSILON))).astype(jnp.bfloat16)
    unit_wide = unit.astype(jnp.float32)
    slot_iota = jnp.arange(KP, dtype=jnp.int32)
    valid = (slot_iota[None, :] < image_counts[:, None]).astype(jnp.float32)
    valid_flat = valid.reshape(-1)
    listed = jnp.zeros((IMAGES, IMAGES), jnp.float32).at[pair_list[:, 0], pair_list[:, 1]].set(1.0)

    def image_rows(image_id):
        rows_unit = lax.dynamic_slice_in_dim(unit_wide, image_id * KP, KP, 0)
        scores = jnp.dot(rows_unit, unit_wide.T, precision=EXACT)
        expo = jnp.exp(SHARPNESS * scores)
        own_valid = lax.dynamic_slice_in_dim(valid, image_id, 1, 0)[0]
        rowsum = lax.optimization_barrier(jnp.sum((expo * valid_flat[None, :]).reshape(KP, IMAGES, KP), axis=2))
        colsum = lax.optimization_barrier(jnp.sum(expo * own_valid[:, None], axis=0))
        present = lax.dynamic_slice_in_dim(listed, image_id, 1, 0)[0]
        denom = jnp.repeat(rowsum, KP, axis=1) * colsum[None, :]
        return KP * expo * own_valid[:, None] * valid_flat[None, :] / jnp.sqrt(denom) * jnp.repeat(present, KP)[None, :]
    matches = lax.map(image_rows, jnp.arange(IMAGES, dtype=jnp.int32)).reshape(KEYPOINTS, KEYPOINTS)
    solution = warm_start.astype(jnp.float32)
    dual = jnp.zeros_like(solution)
    right = factor_init
    identity = jnp.eye(RANK, dtype=jnp.float32)
    for sweep_index in range(ITERS):
        target = solution - dual / PENALTY
        gram_right = jnp.dot(right.T, right, precision=EXACT) + RIDGE * identity
        left = ridge_apply(jnp.dot(target, right, precision=EXACT), gram_right)
        gram_left = jnp.dot(left.T, left, precision=EXACT) + RIDGE * identity
        right = ridge_apply(jnp.dot(target.T, left, precision=EXACT), gram_left)
        lowrank = jnp.dot(left, right.T, precision=EXACT)
        solution = jnp.clip(lowrank + (matches + dual) / PENALTY, 0.0, 1.0)
        dual = dual + PENALTY * (solution - lowrank)
    return (solution.astype(jnp.bfloat16), dual)
```

```python
import functools

import jax
import jax.numpy as jnp
from jax import lax
from jax.experimental import pallas as pl
from jax.experimental.pallas import tpu as pltpu
from jax.sharding import PartitionSpec as P

KP = 256

EPSILON = 1e-06
SHARPNESS = 10.0
RIDGE = 16.0
EXACT = lax.Precision.HIGHEST
F32 = jnp.float32
BF16 = jnp.bfloat16
PARAMS = pltpu.CompilerParams(vmem_limit_bytes=48 * 1024 * 1024)
SETTLED = 2e-4


def halves(x):
    high = x.astype(BF16)
    return high, (x - high.astype(F32)).astype(BF16)


def dot32(a, b):
    return jnp.dot(a, b, preferred_element_type=F32)


def exact(a, b):
    return jnp.dot(a, b, precision=EXACT, preferred_element_type=F32)


def eye(n):
    return (
        lax.broadcasted_iota(jnp.int32, (n, n), 0) == lax.broadcasted_iota(jnp.int32, (n, n), 1)
    ).astype(F32)


def invert(matrix_ref, inverse_ref):
    n = matrix_ref.shape[0]
    top = jnp.max(jnp.sum(jnp.abs(matrix_ref[...]), axis=1, keepdims=True))
    inverse_ref[...] = (2.0 / (RIDGE + top)) * eye(n)

    def step(spread):
        scale = 2.0 / (2.0 - spread * spread)
        rest = (2.0 * scale) * eye(n) - scale * exact(matrix_ref[...], inverse_ref[...])
        inverse_ref[...] = exact(inverse_ref[...], rest)
        return spread * spread / (2.0 - spread * spread)

    spread = lax.while_loop(lambda s: s > SETTLED, step, (top - RIDGE) / (top + RIDGE))
    step(spread)


def inverse_body(gram_ref, out_ref, matrix_ref):
    matrix_ref[...] = gram_ref[...] + RIDGE * eye(gram_ref.shape[0])
    invert(matrix_ref, out_ref)


def ridge_inverse(gram):
    return pl.pallas_call(
        inverse_body,
        out_shape=jax.ShapeDtypeStruct(gram.shape, F32),
        scratch_shapes=[pltpu.VMEM(gram.shape, F32)],
        compiler_params=PARAMS,
        name="ridge_inverse",
        cost_estimate=pl.CostEstimate(flops=200 * gram.shape[0] ** 3, bytes_accessed=8 * gram.size, transcendentals=0),
    )(gram)


def second_body(gram_right_ref, gram_left_ref, out_ref, matrix_ref, inverse_ref, filter_ref):
    n = out_ref.shape[0]
    matrix_ref[...] = gram_right_ref[...] + RIDGE * eye(n)
    invert(matrix_ref, inverse_ref)
    filter_ref[...] = eye(n) - RIDGE * inverse_ref[...]
    out_ref[...] = exact(filter_ref[...], gram_left_ref[...])
    matrix_ref[...] = exact(out_ref[...], filter_ref[...]) + RIDGE * eye(n)
    invert(matrix_ref, inverse_ref)
    out_ref[...] = exact(exact(filter_ref[...], inverse_ref[...]), out_ref[...])


def second_mix(gram_right, gram_left):
    n = gram_right.shape[0]
    return pl.pallas_call(
        second_body,
        out_shape=jax.ShapeDtypeStruct((n, n), F32),
        scratch_shapes=[pltpu.VMEM((n, n), F32)] * 3,
        compiler_params=PARAMS,
        name="second_mix",
        cost_estimate=pl.CostEstimate(flops=400 * n**3, bytes_accessed=12 * n * n, transcendentals=0),
    )(gram_right, gram_left)


def left_sum_body(warm_ref, right_ref, out_ref, high_ref, low_ref):
    @pl.when(pl.program_id(0) == 0)
    def _():
        high_ref[...], low_ref[...] = halves(right_ref[...])

    out_ref[...] = dot32(warm_ref[...], high_ref[...]) + dot32(warm_ref[...], low_ref[...])


def left_sum(warm, right):
    rows, cols = warm.shape
    rank = right.shape[1]
    return pl.pallas_call(
        left_sum_body,
        grid=(rows // KP,),
        in_specs=[
            pl.BlockSpec((KP, cols), lambda i: (i, 0)),
            pl.BlockSpec((cols, rank), lambda i: (0, 0)),
        ],
        out_specs=pl.BlockSpec((KP, rank), lambda i: (i, 0)),
        out_shape=jax.ShapeDtypeStruct((rows, rank), F32),
        scratch_shapes=[pltpu.VMEM((cols, rank), BF16)] * 2,
        compiler_params=PARAMS,
        name="left_sum",
        cost_estimate=pl.CostEstimate(flops=4 * rows * cols * rank, bytes_accessed=2 * rows * cols, transcendentals=0),
    )(warm, right)


def right_sum_body(left_ref, warm_ref, out_ref, turned_ref):
    rank = out_ref.shape[0]

    @pl.when(pl.program_id(0) == 0)
    def _():
        turned_ref[...] = left_ref[...].T

    out_ref[...] = dot32(turned_ref[:rank, :], warm_ref[...]) + dot32(turned_ref[rank:, :], warm_ref[...])


def right_sum(left_pair, warm):
    rows, cols = warm.shape
    rank = left_pair.shape[1] // 2
    return pl.pallas_call(
        right_sum_body,
        grid=(cols // KP,),
        in_specs=[
            pl.BlockSpec((rows, 2 * rank), lambda i: (0, 0)),
            pl.BlockSpec((rows, KP), lambda i: (0, i)),
        ],
        out_specs=pl.BlockSpec((rank, KP), lambda i: (0, i)),
        out_shape=jax.ShapeDtypeStruct((rank, cols), F32),
        scratch_shapes=[pltpu.VMEM((2 * rank, rows), BF16)],
        compiler_params=PARAMS,
        name="right_sum",
        cost_estimate=pl.CostEstimate(flops=4 * rows * cols * rank, bytes_accessed=2 * rows * cols, transcendentals=0),
    )(left_pair, warm)


def left_apply_body(terms_ref, inverse_ref, pair_ref, gram_ref):
    rank = terms_ref.shape[1]
    left = exact(terms_ref[...], inverse_ref[...])
    high, low = halves(left)
    pair_ref[:, :rank] = high
    pair_ref[:, rank:] = low
    gram_ref[...] = exact(left.T, left)


def left_apply(terms, inverse):
    rows, rank = terms.shape
    return pl.pallas_call(
        left_apply_body,
        out_shape=(jax.ShapeDtypeStruct((rows, 2 * rank), BF16), jax.ShapeDtypeStruct((rank, rank), F32)),
        compiler_params=PARAMS,
        name="left_apply",
    )(terms, inverse)


def right_apply_body(terms_ref, inverse_ref, pair_ref, gram_ref):
    rank = terms_ref.shape[0]
    right = exact(inverse_ref[...], terms_ref[...])
    high, low = halves(right)
    pair_ref[:rank, :] = high
    pair_ref[rank:, :] = low
    gram_ref[...] = exact(right, right.T)


def right_apply(terms, inverse):
    rank, cols = terms.shape
    return pl.pallas_call(
        right_apply_body,
        out_shape=(jax.ShapeDtypeStruct((2 * rank, cols), BF16), jax.ShapeDtypeStruct((rank, rank), F32)),
        compiler_params=PARAMS,
        name="right_apply",
    )(terms, inverse)


def finish_body(
    img_col,
    present_ref, row_count_ref, col_count_ref,
    row_unit_ref, col_unit_ref, left_ref, right_ref, mix_ref,
    assign_ref, dual_ref,
    second_ref, match_ref,
):
    rank = mix_ref.shape[0]
    step = pl.program_id(0)

    @pl.when(step == 0)
    def _():
        mix_high, mix_low = halves(mix_ref[...])
        high, low = right_ref[:rank, :], right_ref[rank:, :]
        mixed = dot32(mix_high, high) + dot32(mix_low, high) + dot32(mix_high, low)
        second_ref[:rank, :], second_ref[rank:, :] = halves(mixed)

    row_valid = lax.broadcasted_iota(jnp.int32, (KP, 1), 0) < row_count_ref[step]
    for image in range(img_col):
        cell = slice(image * KP, (image + 1) * KP)
        listed = present_ref[step * img_col + image] > 0

        @pl.when(listed)
        def _():
            scores = lax.dot_general(
                row_unit_ref[...], col_unit_ref[cell, :], (((1,), (1,)), ((), ())), preferred_element_type=F32
            )
            expo = jnp.exp(SHARPNESS * scores)
            col_valid = lax.broadcasted_iota(jnp.int32, (1, KP), 1) < col_count_ref[image]
            by_col = jnp.where(col_valid, expo, 0.0)
            by_row = jnp.where(row_valid, expo, 0.0)
            rowsum = jnp.sum(by_col, axis=1, keepdims=True)
            colsum = jnp.sum(by_row, axis=0, keepdims=True)
            both = jnp.where(row_valid, by_col, 0.0)
            match_ref[:, cell] = both * ((0.5 * KP) * lax.rsqrt(rowsum)) * lax.rsqrt(colsum)

        @pl.when(jnp.logical_not(listed))
        def _():
            match_ref[:, cell] = jnp.zeros((KP, KP), F32)

        left_high, left_low = left_ref[:, :rank], left_ref[:, rank:]

        def product(ref):
            high = ref[:rank, cell]
            return dot32(left_high, high) + dot32(left_high, ref[rank:, cell]) + dot32(left_low, high)

        half_match = match_ref[:, cell]
        lowrank = product(right_ref)
        half_dual = jnp.clip(lowrank + half_match, 0.0, 1.0) - lowrank
        lowrank = product(second_ref)
        solution = jnp.clip(lowrank + (half_match + half_dual), 0.0, 1.0)
        dual_ref[:, cell] = 2.0 * (half_dual + (solution - lowrank))
        assign_ref[:, cell] = solution.astype(BF16)


def finish(present, row_count, col_count, row_unit, col_unit, left_pair, right_pair, mix):
    rows, rank = left_pair.shape[0], mix.shape[0]
    cols = right_pair.shape[1]
    img_col = cols // KP
    smem = pl.BlockSpec(memory_space=pltpu.SMEM)
    return pl.pallas_call(
        functools.partial(finish_body, img_col),
        grid=(rows // KP,),
        in_specs=[
            smem, smem, smem,
            pl.BlockSpec((KP, row_unit.shape[1]), lambda i: (i, 0)),
            pl.BlockSpec(col_unit.shape, lambda i: (0, 0)),
            pl.BlockSpec((KP, 2 * rank), lambda i: (i, 0)),
            pl.BlockSpec((2 * rank, cols), lambda i: (0, 0)),
            pl.BlockSpec((rank, rank), lambda i: (0, 0)),
        ],
        out_specs=(pl.BlockSpec((KP, cols), lambda i: (i, 0)), pl.BlockSpec((KP, cols), lambda i: (i, 0))),
        out_shape=(jax.ShapeDtypeStruct((rows, cols), BF16), jax.ShapeDtypeStruct((rows, cols), F32)),
        scratch_shapes=[pltpu.VMEM((2 * rank, cols), BF16), pltpu.VMEM((KP, cols), F32)],
        compiler_params=PARAMS,
        name="finish",
        cost_estimate=pl.CostEstimate(flops=12 * rows * cols * rank, bytes_accessed=6 * rows * cols, transcendentals=rows * cols),
    )(present, row_count, col_count, row_unit, col_unit, left_pair, right_pair, mix)


def local(descriptors, image_counts, pair_list, warm_start, factor_init):
    row_place = lax.axis_index("row")
    col_place = lax.axis_index("col")
    rows, cols = warm_start.shape
    img_row, img_col = rows // KP, cols // KP

    left_terms = left_sum(warm_start, factor_init)
    gram_right = lax.psum(lax.dot_general(factor_init, factor_init, (((0,), (0,)), ((), ())), precision=EXACT), "col")
    left_terms = lax.psum_scatter(left_terms, "col", scatter_dimension=0, tiled=True)

    wide = descriptors.astype(F32)
    unit = (
        wide * lax.rsqrt(descriptors.shape[1] * (jnp.mean(wide * wide, axis=1, keepdims=True) + EPSILON))
    ).astype(BF16)
    everyone = lax.all_gather(unit, "row", axis=0, tiled=True)
    col_unit = lax.dynamic_slice_in_dim(everyone, col_place * cols, cols, 0)
    listed = lax.all_gather(pair_list, "col", axis=0, tiled=True)
    in_block = listed[:, 1] // img_col == col_place
    local_code = (listed[:, 0] - img_row * row_place) * img_col + (listed[:, 1] - img_col * col_place)
    cell_iota = jnp.arange(img_row * img_col, dtype=jnp.int32)
    present = jnp.any((local_code[:, None] == cell_iota[None, :]) & in_block[:, None], axis=0).astype(jnp.int32)
    row_count = lax.dynamic_slice_in_dim(image_counts, row_place * img_row, img_row, 0)
    col_count = lax.dynamic_slice_in_dim(image_counts, col_place * img_col, img_col, 0)

    left_pair, gram_left = left_apply(left_terms, ridge_inverse(gram_right))
    gram_left = lax.psum(gram_left, ("row", "col"))
    left_pair = lax.all_gather(left_pair, "col", axis=0, tiled=True)
    right_terms = lax.psum_scatter(right_sum(left_pair, warm_start), "row", scatter_dimension=1, tiled=True)
    right_pair, gram_right = right_apply(right_terms, ridge_inverse(gram_left))
    gram_right = lax.psum(gram_right, ("row", "col"))
    right_pair = lax.all_gather(right_pair, "row", axis=1, tiled=True)
    mix = second_mix(gram_right, gram_left)
    return finish(present, row_count, col_count, unit, col_unit, left_pair, right_pair, mix)


def solution(mesh):
    return jax.shard_map(
        local,
        mesh=mesh,
        in_specs=(P("row", None), P(), P(("row", "col"), None), P("row", "col"), P("col", None)),
        out_specs=(P("row", "col"), P("row", "col")),
        check_vma=False,
    )
```

```python
import functools

import jax
import jax.numpy as jnp
from jax import lax
from jax.experimental import pallas as pl
from jax.experimental.pallas import tpu as pltpu
from jax.sharding import PartitionSpec as P

KP = 256

EPSILON = 1e-06
SHARPNESS = 10.0
RIDGE = 16.0
EXACT = lax.Precision.HIGHEST
F32 = jnp.float32
BF16 = jnp.bfloat16
PARAMS = pltpu.CompilerParams(vmem_limit_bytes=48 * 1024 * 1024)
SETTLED = 2e-4


def halves(x):
    high = x.astype(BF16)
    return high, (x - high.astype(F32)).astype(BF16)


def dot32(a, b):
    return jnp.dot(a, b, preferred_element_type=F32)


def exact(a, b):
    return jnp.dot(a, b, precision=EXACT, preferred_element_type=F32)


def eye(n):
    return (
        lax.broadcasted_iota(jnp.int32, (n, n), 0) == lax.broadcasted_iota(jnp.int32, (n, n), 1)
    ).astype(F32)


def invert(matrix_ref, inverse_ref):
    n = matrix_ref.shape[0]
    top = jnp.max(jnp.sum(jnp.abs(matrix_ref[...]), axis=1, keepdims=True))
    inverse_ref[...] = (2.0 / (RIDGE + top)) * eye(n)

    def step(spread):
        scale = 2.0 / (2.0 - spread * spread)
        rest = (2.0 * scale) * eye(n) - scale * exact(matrix_ref[...], inverse_ref[...])
        inverse_ref[...] = exact(inverse_ref[...], rest)
        return spread * spread / (2.0 - spread * spread)

    spread = lax.while_loop(lambda s: s > SETTLED, step, (top - RIDGE) / (top + RIDGE))
    step(spread)


def inverse_body(gram_ref, out_ref, matrix_ref):
    matrix_ref[...] = gram_ref[...] + RIDGE * eye(gram_ref.shape[0])
    invert(matrix_ref, out_ref)


def ridge_inverse(gram):
    return pl.pallas_call(
        inverse_body,
        out_shape=jax.ShapeDtypeStruct(gram.shape, F32),
        scratch_shapes=[pltpu.VMEM(gram.shape, F32)],
        compiler_params=PARAMS,
        name="ridge_inverse",
        cost_estimate=pl.CostEstimate(flops=200 * gram.shape[0] ** 3, bytes_accessed=8 * gram.size, transcendentals=0),
    )(gram)


def second_body(gram_right_ref, gram_left_ref, out_ref, matrix_ref, inverse_ref, filter_ref):
    n = out_ref.shape[0]
    matrix_ref[...] = gram_right_ref[...] + RIDGE * eye(n)
    invert(matrix_ref, inverse_ref)
    filter_ref[...] = eye(n) - RIDGE * inverse_ref[...]
    out_ref[...] = exact(filter_ref[...], gram_left_ref[...])
    matrix_ref[...] = exact(out_ref[...], filter_ref[...]) + RIDGE * eye(n)
    invert(matrix_ref, inverse_ref)
    out_ref[...] = exact(exact(filter_ref[...], inverse_ref[...]), out_ref[...])


def second_mix(gram_right, gram_left):
    n = gram_right.shape[0]
    return pl.pallas_call(
        second_body,
        out_shape=jax.ShapeDtypeStruct((n, n), F32),
        scratch_shapes=[pltpu.VMEM((n, n), F32)] * 3,
        compiler_params=PARAMS,
        name="second_mix",
        cost_estimate=pl.CostEstimate(flops=400 * n**3, bytes_accessed=12 * n * n, transcendentals=0),
    )(gram_right, gram_left)


def left_sum_body(warm_ref, right_ref, out_ref, high_ref, low_ref):
    @pl.when(pl.program_id(0) == 0)
    def _():
        high_ref[...], low_ref[...] = halves(right_ref[...])

    out_ref[...] = dot32(warm_ref[...], high_ref[...]) + dot32(warm_ref[...], low_ref[...])


def left_sum(warm, right):
    rows, cols = warm.shape
    rank = right.shape[1]
    return pl.pallas_call(
        left_sum_body,
        grid=(rows // KP,),
        in_specs=[
            pl.BlockSpec((KP, cols), lambda i: (i, 0)),
            pl.BlockSpec((cols, rank), lambda i: (0, 0)),
        ],
        out_specs=pl.BlockSpec((KP, rank), lambda i: (i, 0)),
        out_shape=jax.ShapeDtypeStruct((rows, rank), F32),
        scratch_shapes=[pltpu.VMEM((cols, rank), BF16)] * 2,
        compiler_params=PARAMS,
        name="left_sum",
        cost_estimate=pl.CostEstimate(flops=4 * rows * cols * rank, bytes_accessed=2 * rows * cols, transcendentals=0),
    )(warm, right)


def right_sum_body(left_ref, warm_ref, out_ref, turned_ref):
    rank = out_ref.shape[0]

    @pl.when(pl.program_id(0) == 0)
    def _():
        turned_ref[...] = left_ref[...].T

    out_ref[...] = dot32(turned_ref[:rank, :], warm_ref[...]) + dot32(turned_ref[rank:, :], warm_ref[...])


def right_sum(left_pair, warm):
    rows, cols = warm.shape
    rank = left_pair.shape[1] // 2
    return pl.pallas_call(
        right_sum_body,
        grid=(cols // KP,),
        in_specs=[
            pl.BlockSpec((rows, 2 * rank), lambda i: (0, 0)),
            pl.BlockSpec((rows, KP), lambda i: (0, i)),
        ],
        out_specs=pl.BlockSpec((rank, KP), lambda i: (0, i)),
        out_shape=jax.ShapeDtypeStruct((rank, cols), F32),
        scratch_shapes=[pltpu.VMEM((2 * rank, rows), BF16)],
        compiler_params=PARAMS,
        name="right_sum",
        cost_estimate=pl.CostEstimate(flops=4 * rows * cols * rank, bytes_accessed=2 * rows * cols, transcendentals=0),
    )(left_pair, warm)


def left_apply_body(terms_ref, inverse_ref, pair_ref, gram_ref):
    rank = terms_ref.shape[1]
    left = exact(terms_ref[...], inverse_ref[...])
    high, low = halves(left)
    pair_ref[:, :rank] = high
    pair_ref[:, rank:] = low
    gram_ref[...] = exact(left.T, left)


def left_apply(terms, inverse):
    rows, rank = terms.shape
    return pl.pallas_call(
        left_apply_body,
        out_shape=(jax.ShapeDtypeStruct((rows, 2 * rank), BF16), jax.ShapeDtypeStruct((rank, rank), F32)),
        compiler_params=PARAMS,
        name="left_apply",
    )(terms, inverse)


def right_apply_body(terms_ref, inverse_ref, pair_ref, gram_ref):
    rank = terms_ref.shape[0]
    right = exact(inverse_ref[...], terms_ref[...])
    high, low = halves(right)
    pair_ref[:rank, :] = high
    pair_ref[rank:, :] = low
    gram_ref[...] = exact(right, right.T)


def right_apply(terms, inverse):
    rank, cols = terms.shape
    return pl.pallas_call(
        right_apply_body,
        out_shape=(jax.ShapeDtypeStruct((2 * rank, cols), BF16), jax.ShapeDtypeStruct((rank, rank), F32)),
        compiler_params=PARAMS,
        name="right_apply",
    )(terms, inverse)


def finish_body(
    img_col,
    present_ref, row_count_ref, col_count_ref,
    row_unit_ref, col_unit_ref, left_ref, right_ref, mix_ref,
    assign_ref, dual_ref,
    second_ref, match_ref,
):
    rank = mix_ref.shape[0]
    step = pl.program_id(0)

    @pl.when(step == 0)
    def _():
        mix_high, mix_low = halves(mix_ref[...])
        high, low = right_ref[:rank, :], right_ref[rank:, :]
        mixed = dot32(mix_high, high) + dot32(mix_low, high) + dot32(mix_high, low)
        second_ref[:rank, :], second_ref[rank:, :] = halves(mixed)

    row_valid = lax.broadcasted_iota(jnp.int32, (KP, 1), 0) < row_count_ref[step]
    for image in range(img_col):
        cell = slice(image * KP, (image + 1) * KP)
        listed = present_ref[step * img_col + image] > 0

        @pl.when(listed)
        def _():
            scores = lax.dot_general(
                row_unit_ref[...], col_unit_ref[cell, :], (((1,), (1,)), ((), ())), preferred_element_type=F32
            )
            expo = jnp.exp(SHARPNESS * scores)
            col_valid = lax.broadcasted_iota(jnp.int32, (1, KP), 1) < col_count_ref[image]
            by_col = jnp.where(col_valid, expo, 0.0)
            by_row = jnp.where(row_valid, expo, 0.0)
            rowsum = jnp.sum(by_col, axis=1, keepdims=True)
            colsum = jnp.sum(by_row, axis=0, keepdims=True)
            both = jnp.where(row_valid, by_col, 0.0)
            match_ref[:, cell] = both * ((0.5 * KP) * lax.rsqrt(rowsum)) * lax.rsqrt(colsum)

        @pl.when(jnp.logical_not(listed))
        def _():
            match_ref[:, cell] = jnp.zeros((KP, KP), F32)

        left_high, left_low = left_ref[:, :rank], left_ref[:, rank:]

        def product(ref):
            high = ref[:rank, cell]
            return dot32(left_high, high) + dot32(left_high, ref[rank:, cell]) + dot32(left_low, high)

        half_match = match_ref[:, cell]
        lowrank = product(right_ref)
        half_dual = jnp.clip(lowrank + half_match, 0.0, 1.0) - lowrank
        lowrank = product(second_ref)
        solution = jnp.clip(lowrank + (half_match + half_dual), 0.0, 1.0)
        dual_ref[:, cell] = 2.0 * (half_dual + (solution - lowrank))
        assign_ref[:, cell] = solution.astype(BF16)


def finish(present, row_count, col_count, row_unit, col_unit, left_pair, right_pair, mix):
    rows, rank = left_pair.shape[0], mix.shape[0]
    cols = right_pair.shape[1]
    img_col = cols // KP
    smem = pl.BlockSpec(memory_space=pltpu.SMEM)
    return pl.pallas_call(
        functools.partial(finish_body, img_col),
        grid=(rows // KP,),
        in_specs=[
            smem, smem, smem,
            pl.BlockSpec((KP, row_unit.shape[1]), lambda i: (i, 0)),
            pl.BlockSpec(col_unit.shape, lambda i: (0, 0)),
            pl.BlockSpec((KP, 2 * rank), lambda i: (i, 0)),
            pl.BlockSpec((2 * rank, cols), lambda i: (0, 0)),
            pl.BlockSpec((rank, rank), lambda i: (0, 0)),
        ],
        out_specs=(pl.BlockSpec((KP, cols), lambda i: (i, 0)), pl.BlockSpec((KP, cols), lambda i: (i, 0))),
        out_shape=(jax.ShapeDtypeStruct((rows, cols), BF16), jax.ShapeDtypeStruct((rows, cols), F32)),
        scratch_shapes=[pltpu.VMEM((2 * rank, cols), BF16), pltpu.VMEM((KP, cols), F32)],
        compiler_params=PARAMS,
        name="finish",
        cost_estimate=pl.CostEstimate(flops=12 * rows * cols * rank, bytes_accessed=6 * rows * cols, transcendentals=rows * cols),
    )(present, row_count, col_count, row_unit, col_unit, left_pair, right_pair, mix)


MESH = pl.DeviceIdType.MESH


def greet(peers):
    barrier = pltpu.get_barrier_semaphore()
    for peer in peers:
        pl.semaphore_signal(barrier, inc=1, device_id=peer, device_id_type=MESH)
    pl.semaphore_wait(barrier, len(peers))


def ring_place(place, step, total):
    return lax.rem(place + step, total)


def sum_body(
    over_rows, row_total, col_total,
    part_ref, out_ref, extra_ref,
    col_in, row_in, spread, send_col, recv_col, send_row, recv_row, send_out, recv_out,
):
    row, col = lax.axis_index("row"), lax.axis_index("col")
    piece = spread.shape[1]
    cols = [(row, ring_place(col, k, col_total)) for k in range(1, col_total)]
    rows = [(ring_place(row, k, row_total), col) for k in range(1, row_total)] if over_rows else []
    greet(cols + rows)
    copies = []
    for k in range(1, col_total):
        copy = pltpu.make_async_remote_copy(
            src_ref=part_ref.at[cols[k - 1][1]], dst_ref=col_in.at[k - 1],
            send_sem=send_col.at[k - 1], recv_sem=recv_col.at[k - 1],
            device_id=cols[k - 1], device_id_type=MESH,
        )
        copy.start()
        copies.append(copy)
    total = part_ref[col]
    for k in range(1, col_total):
        copies[k - 1].wait_recv()
        total = total + col_in[k - 1]
    if extra_ref.shape[0] != 0:
        extra_ref[...] = total[piece:, :]
        total = total[:piece, :]
    if over_rows:
        row_in[row] = total
        for k in range(1, row_total):
            copy = pltpu.make_async_remote_copy(
                src_ref=row_in.at[row], dst_ref=row_in.at[row],
                send_sem=send_row.at[k - 1], recv_sem=recv_row.at[k - 1],
                device_id=rows[k - 1], device_id_type=MESH,
            )
            copy.start()
            copies.append(copy)
        for copy in copies[col_total - 1:]:
            copy.wait_recv()
        total = row_in[0]
        for k in range(1, row_total):
            total = total + row_in[k]
    spread[col] = total
    last = []
    for k in range(1, col_total):
        copy = pltpu.make_async_remote_copy(
            src_ref=spread.at[col], dst_ref=spread.at[col],
            send_sem=send_out.at[k - 1], recv_sem=recv_out.at[k - 1],
            device_id=cols[k - 1], device_id_type=MESH,
        )
        copy.start()
        last.append(copy)
    for copy in last:
        copy.wait_recv()
    out_ref[...] = spread[...]
    for copy in copies + last:
        copy.wait_send()


def sum_everywhere(part, extra, over_rows, call_id, name):
    n = part.shape[0]
    row_total, col_total = lax.axis_size("row"), lax.axis_size("col")
    piece = n // col_total
    stacked = jnp.concatenate([part.reshape(col_total, piece, n), extra], axis=1)
    dma = pltpu.SemaphoreType.DMA
    total, rest = pl.pallas_call(
        functools.partial(sum_body, over_rows, row_total, col_total),
        in_specs=[pl.BlockSpec(memory_space=pltpu.VMEM)],
        out_specs=(pl.BlockSpec(memory_space=pltpu.VMEM),) * 2,
        out_shape=(
            jax.ShapeDtypeStruct((col_total, piece, n), F32),
            jax.ShapeDtypeStruct((extra.shape[1], n), F32),
        ),
        scratch_shapes=[
            pltpu.VMEM((col_total - 1, piece + extra.shape[1], n), F32),
            pltpu.VMEM((row_total, piece, n), F32),
            pltpu.VMEM((col_total, piece, n), F32),
            dma((col_total - 1,)), dma((col_total - 1,)),
            dma((row_total - 1,)), dma((row_total - 1,)),
            dma((col_total - 1,)), dma((col_total - 1,)),
        ],
        compiler_params=pltpu.CompilerParams(
            vmem_limit_bytes=48 * 1024 * 1024, collective_id=call_id, has_side_effects=True
        ),
        name=name,
        cost_estimate=pl.CostEstimate(flops=n * n * 10, bytes_accessed=40 * n * n, transcendentals=0),
    )(stacked)
    return total.reshape(n, n), rest


def chip_peers(col_total):
    row, col = lax.axis_index("row"), lax.axis_index("col")
    core = lax.rem(col, 2)
    chips = col_total // 2
    chip = col // 2
    sibling = (row, col + 1 - 2 * core)
    ahead = [(row, 2 * ring_place(chip, k, chips) + core) for k in range(1, chips)]
    return row, col, core, chip, chips, sibling, ahead


def reduce_body(col_total, terms_ref, out_ref, from_core, joined, from_chip, send_core, recv_core, send_chip, recv_chip):
    row, col, core, chip, chips, sibling, ahead = chip_peers(col_total)
    greet([sibling] + ahead)
    order = list(range(1, chips)) + [0]
    near, far = {}, {}
    for k in order:
        copy = pltpu.make_async_remote_copy(
            src_ref=terms_ref.at[2 * ring_place(chip, k, chips) + 1 - core], dst_ref=from_core.at[k],
            send_sem=send_core.at[k], recv_sem=recv_core.at[k], device_id=sibling, device_id_type=MESH,
        )
        copy.start()
        near[k] = copy
    for k in order[:-1]:
        near[k].wait_recv()
        joined[k - 1] = terms_ref[2 * ring_place(chip, k, chips) + core] + from_core[k]
        copy = pltpu.make_async_remote_copy(
            src_ref=joined.at[k - 1], dst_ref=from_chip.at[k - 1],
            send_sem=send_chip.at[k - 1], recv_sem=recv_chip.at[k - 1],
            device_id=ahead[k - 1], device_id_type=MESH,
        )
        copy.start()
        far[k] = copy
    near[0].wait_recv()
    total = terms_ref[col] + from_core[0]
    for k in order[:-1]:
        far[k].wait_recv()
        total = total + from_chip[k - 1]
    out_ref[...] = total
    for copy in list(near.values()) + list(far.values()):
        copy.wait_send()


def reduce_over_col(terms, call_id):
    rows, rank = terms.shape
    col_total = lax.axis_size("col")
    chips = col_total // 2
    piece = rows // col_total
    dma = pltpu.SemaphoreType.DMA
    return pl.pallas_call(
        functools.partial(reduce_body, col_total),
        in_specs=[pl.BlockSpec(memory_space=pltpu.VMEM)],
        out_specs=pl.BlockSpec(memory_space=pltpu.VMEM),
        out_shape=jax.ShapeDtypeStruct((piece, rank), F32),
        scratch_shapes=[
            pltpu.VMEM((chips, piece, rank), F32),
            pltpu.VMEM((chips - 1, piece, rank), F32),
            pltpu.VMEM((chips - 1, piece, rank), F32),
            dma((chips,)), dma((chips,)), dma((chips - 1,)), dma((chips - 1,)),
        ],
        compiler_params=pltpu.CompilerParams(
            vmem_limit_bytes=48 * 1024 * 1024, collective_id=call_id, has_side_effects=True
        ),
        name="left_reduce",
        cost_estimate=pl.CostEstimate(flops=rows * rank, bytes_accessed=40 * rows * rank, transcendentals=0),
    )(terms.reshape(col_total, piece, rank))


def gather_body(col_total, piece_ref, out_ref, held, send_core, recv_core, send_chip, recv_chip):
    row, col, core, chip, chips, sibling, ahead = chip_peers(col_total)
    held[col] = piece_ref[...]
    greet([sibling] + ahead)

    def send(slot, target, send_sem, recv_sem):
        copy = pltpu.make_async_remote_copy(
            src_ref=held.at[slot], dst_ref=held.at[slot], send_sem=send_sem, recv_sem=recv_sem,
            device_id=target, device_id_type=MESH,
        )
        copy.start()
        return copy

    far = [send(col, ahead[k - 1], send_chip.at[k - 1], recv_chip.at[k - 1]) for k in range(1, chips)]
    near = [send(col, sibling, send_core.at[0], recv_core.at[0])]
    for k in range(1, chips):
        far[k - 1].wait_recv()
        source = 2 * ring_place(chip, chips - k, chips) + core
        near.append(send(source, sibling, send_core.at[k], recv_core.at[k]))
    for copy in near:
        copy.wait_recv()
    out_ref[...] = held[...]
    for copy in near + far:
        copy.wait_send()


def gather_over_col(piece, call_id):
    rows, width = piece.shape
    col_total = lax.axis_size("col")
    chips = col_total // 2
    dma = pltpu.SemaphoreType.DMA
    whole = pl.pallas_call(
        functools.partial(gather_body, col_total),
        in_specs=[pl.BlockSpec(memory_space=pltpu.VMEM)],
        out_specs=pl.BlockSpec(memory_space=pltpu.VMEM),
        out_shape=jax.ShapeDtypeStruct((col_total, rows, width), piece.dtype),
        scratch_shapes=[
            pltpu.VMEM((col_total, rows, width), piece.dtype),
            dma((chips,)), dma((chips,)), dma((chips - 1,)), dma((chips - 1,)),
        ],
        compiler_params=pltpu.CompilerParams(
            vmem_limit_bytes=48 * 1024 * 1024, collective_id=call_id, has_side_effects=True
        ),
        name="left_gather",
        cost_estimate=pl.CostEstimate(flops=rows, bytes_accessed=80 * rows * width, transcendentals=0),
    )(piece)
    return whole.reshape(col_total * rows, width)


def own_columns(unit, cols):
    rows = unit.shape[0]
    row_total, col_total = lax.axis_size("row"), lax.axis_size("col")
    start = lax.axis_index("col") * cols
    held = lax.dynamic_slice_in_dim(unit, lax.rem(start, rows), cols, 0)
    found = jnp.where(start // rows == lax.axis_index("row"), held, jnp.zeros_like(held))
    for k in range(1, row_total):
        pairs = []
        for place in range(col_total):
            owner = place * cols // rows
            pairs.append((owner * col_total + place, (owner + k) % row_total * col_total + place))
        found = found + lax.ppermute(held, ("row", "col"), pairs)
    return found


def local(descriptors, image_counts, pair_list, warm_start, factor_init):
    row_place = lax.axis_index("row")
    col_place = lax.axis_index("col")
    rows, cols = warm_start.shape
    img_row, img_col = rows // KP, cols // KP

    row_total, col_total = lax.axis_size("row"), lax.axis_size("col")
    rank = factor_init.shape[1]

    cells = img_row * img_col
    codes = (pair_list[:, 0] - img_row * row_place) * img_col + lax.rem(pair_list[:, 1], img_col)
    hits = (pair_list[:, 1] // img_col)[:, None] == jnp.arange(col_total, dtype=jnp.int32)[None, :]
    marks = codes[:, None] == jnp.arange(cells, dtype=jnp.int32)[None, :]
    flags = jnp.any(hits[:, :, None] & marks[:, None, :], axis=0).astype(F32)
    flags = jnp.pad(flags[:, None, :], ((0, 0), (0, 7), (0, rank - cells)))
    blank = jnp.zeros((col_total, 8, rank), F32)

    left_terms = left_sum(warm_start, factor_init)
    gram_right = lax.dot_general(factor_init, factor_init, (((0,), (0,)), ((), ())), precision=EXACT)
    gram_right, listed = sum_everywhere(gram_right, flags, False, 1, "start_gram")
    present = (listed[0, :cells] > 0.5).astype(jnp.int32)
    left_terms = reduce_over_col(left_terms, 2)

    wide = descriptors.astype(F32)
    unit = (
        wide * lax.rsqrt(descriptors.shape[1] * (jnp.mean(wide * wide, axis=1, keepdims=True) + EPSILON))
    ).astype(BF16)
    col_unit = own_columns(unit, cols)
    row_count = lax.dynamic_slice_in_dim(image_counts, row_place * img_row, img_row, 0)
    col_count = lax.dynamic_slice_in_dim(image_counts, col_place * img_col, img_col, 0)

    left_pair, gram_left = left_apply(left_terms, ridge_inverse(gram_right))
    left_pair = gather_over_col(left_pair, 3)
    right_terms = right_sum(left_pair, warm_start)
    gram_left, right_terms = lax.optimization_barrier((gram_left, right_terms))
    right_terms = lax.psum_scatter(right_terms, "row", scatter_dimension=1, tiled=True)
    gram_left = sum_everywhere(gram_left, blank, True, 4, "left_gram")[0]
    right_pair, gram_right = right_apply(right_terms, ridge_inverse(gram_left))
    right_pair = lax.all_gather(right_pair, "row", axis=1, tiled=True)
    gram_right = sum_everywhere(gram_right, blank, True, 5, "right_gram")[0]
    mix = second_mix(gram_right, gram_left)
    return finish(present, row_count, col_count, unit, col_unit, left_pair, right_pair, mix)


def solution(mesh):
    return jax.shard_map(
        local,
        mesh=mesh,
        in_specs=(P("row", None), P(), P(("row", "col"), None), P("row", "col"), P("col", None)),
        out_specs=(P("row", "col"), P("row", "col")),
        check_vma=False,
    )
```

```python
import functools

import jax
import jax.numpy as jnp
from jax import lax
from jax.experimental import pallas as pl
from jax.experimental.pallas import tpu as pltpu
from jax.sharding import PartitionSpec as P

KP = 256

EPSILON = 1e-06
SHARPNESS = 10.0
RIDGE = 16.0
EXACT = lax.Precision.HIGHEST
F32 = jnp.float32
BF16 = jnp.bfloat16
PARAMS = pltpu.CompilerParams(vmem_limit_bytes=48 * 1024 * 1024)
SETTLED = 2e-4
ROUGH_TOP = 1000.0 * RIDGE


def halves(x):
    high = x.astype(BF16)
    return high, (x - high.astype(F32)).astype(BF16)


def dot32(a, b):
    return jnp.dot(a, b, preferred_element_type=F32)


def exact(a, b):
    return jnp.dot(a, b, precision=EXACT, preferred_element_type=F32)


def rough_product(a, b):
    a_high, a_low = halves(a)
    b_high, b_low = halves(b)
    return dot32(a_high, b_high) + dot32(a_high, b_low) + dot32(a_low, b_high)


def eye(n):
    return (
        lax.broadcasted_iota(jnp.int32, (n, n), 0) == lax.broadcasted_iota(jnp.int32, (n, n), 1)
    ).astype(F32)


def invert(matrix_ref, inverse_ref):
    n = matrix_ref.shape[0]
    size = jnp.abs(matrix_ref[...])
    top = jnp.max(jnp.sum(size, axis=1, keepdims=True))
    top = jnp.minimum(top, 1.0001 * jnp.sqrt(jnp.sum(jnp.sum(size * size, axis=1, keepdims=True))))
    top = jnp.maximum(top, 1.0001 * RIDGE)
    inverse_ref[...] = (2.0 / (RIDGE + top)) * eye(n)

    def step(product, spread):
        scale = 2.0 / (2.0 - spread * spread)
        rest = (2.0 * scale) * eye(n) - scale * product(matrix_ref[...], inverse_ref[...])
        inverse_ref[...] = product(inverse_ref[...], rest)
        return spread * spread / (2.0 - spread * spread)

    spread = (top - RIDGE) / (top + RIDGE)
    rough = jnp.where(top < ROUGH_TOP, 0.3, 2.0)
    spread = lax.while_loop(lambda s: s > rough, functools.partial(step, rough_product), spread)
    spread = lax.while_loop(lambda s: s > SETTLED, functools.partial(step, exact), spread)
    step(exact, spread)


def inverse_body(gram_ref, out_ref, matrix_ref):
    matrix_ref[...] = gram_ref[...] + RIDGE * eye(gram_ref.shape[0])
    invert(matrix_ref, out_ref)


def ridge_inverse(gram):
    return pl.pallas_call(
        inverse_body,
        out_shape=jax.ShapeDtypeStruct(gram.shape, F32),
        scratch_shapes=[pltpu.VMEM(gram.shape, F32)],
        compiler_params=PARAMS,
        name="ridge_inverse",
        cost_estimate=pl.CostEstimate(flops=200 * gram.shape[0] ** 3, bytes_accessed=8 * gram.size, transcendentals=0),
    )(gram)


def second_body(gram_right_ref, gram_left_ref, out_ref, matrix_ref, inverse_ref, filter_ref):
    n = out_ref.shape[0]
    matrix_ref[...] = gram_right_ref[...] + RIDGE * eye(n)
    invert(matrix_ref, inverse_ref)
    filter_ref[...] = eye(n) - RIDGE * inverse_ref[...]
    out_ref[...] = exact(filter_ref[...], gram_left_ref[...])
    matrix_ref[...] = exact(out_ref[...], filter_ref[...]) + RIDGE * eye(n)
    invert(matrix_ref, inverse_ref)
    out_ref[...] = exact(exact(filter_ref[...], inverse_ref[...]), out_ref[...])


def second_mix(gram_right, gram_left):
    n = gram_right.shape[0]
    return pl.pallas_call(
        second_body,
        out_shape=jax.ShapeDtypeStruct((n, n), F32),
        scratch_shapes=[pltpu.VMEM((n, n), F32)] * 3,
        compiler_params=PARAMS,
        name="second_mix",
        cost_estimate=pl.CostEstimate(flops=400 * n**3, bytes_accessed=12 * n * n, transcendentals=0),
    )(gram_right, gram_left)


def left_sum_body(warm_ref, right_ref, out_ref, high_ref, low_ref):
    @pl.when(pl.program_id(0) == 0)
    def _():
        high_ref[...], low_ref[...] = halves(right_ref[...])

    out_ref[...] = dot32(warm_ref[...], high_ref[...]) + dot32(warm_ref[...], low_ref[...])


def left_sum(warm, right):
    rows, cols = warm.shape
    rank = right.shape[1]
    return pl.pallas_call(
        left_sum_body,
        grid=(rows // KP,),
        in_specs=[
            pl.BlockSpec((KP, cols), lambda i: (i, 0)),
            pl.BlockSpec((cols, rank), lambda i: (0, 0)),
        ],
        out_specs=pl.BlockSpec((KP, rank), lambda i: (i, 0)),
        out_shape=jax.ShapeDtypeStruct((rows, rank), F32),
        scratch_shapes=[pltpu.VMEM((cols, rank), BF16)] * 2,
        compiler_params=PARAMS,
        name="left_sum",
        cost_estimate=pl.CostEstimate(flops=4 * rows * cols * rank, bytes_accessed=2 * rows * cols, transcendentals=0),
    )(warm, right)


def right_sum_body(left_ref, warm_ref, out_ref, turned_ref):
    rank = out_ref.shape[0]

    @pl.when(pl.program_id(0) == 0)
    def _():
        turned_ref[...] = left_ref[...].T

    out_ref[...] = dot32(turned_ref[:rank, :], warm_ref[...]) + dot32(turned_ref[rank:, :], warm_ref[...])


def right_sum(left_pair, warm):
    rows, cols = warm.shape
    rank = left_pair.shape[1] // 2
    return pl.pallas_call(
        right_sum_body,
        grid=(cols // KP,),
        in_specs=[
            pl.BlockSpec((rows, 2 * rank), lambda i: (0, 0)),
            pl.BlockSpec((rows, KP), lambda i: (0, i)),
        ],
        out_specs=pl.BlockSpec((rank, KP), lambda i: (0, i)),
        out_shape=jax.ShapeDtypeStruct((rank, cols), F32),
        scratch_shapes=[pltpu.VMEM((2 * rank, rows), BF16)],
        compiler_params=PARAMS,
        name="right_sum",
        cost_estimate=pl.CostEstimate(flops=4 * rows * cols * rank, bytes_accessed=2 * rows * cols, transcendentals=0),
    )(left_pair, warm)


def left_apply_body(terms_ref, inverse_ref, pair_ref, gram_ref):
    rank = terms_ref.shape[1]
    left = exact(terms_ref[...], inverse_ref[...])
    high, low = halves(left)
    pair_ref[:, :rank] = high
    pair_ref[:, rank:] = low
    gram_ref[...] = exact(left.T, left)


def left_apply(terms, inverse):
    rows, rank = terms.shape
    return pl.pallas_call(
        left_apply_body,
        out_shape=(jax.ShapeDtypeStruct((rows, 2 * rank), BF16), jax.ShapeDtypeStruct((rank, rank), F32)),
        compiler_params=PARAMS,
        name="left_apply",
    )(terms, inverse)


def right_apply_body(terms_ref, inverse_ref, pair_ref, gram_ref):
    rank = terms_ref.shape[0]
    right = exact(inverse_ref[...], terms_ref[...])
    high, low = halves(right)
    pair_ref[:rank, :] = high
    pair_ref[rank:, :] = low
    gram_ref[...] = exact(right, right.T)


def right_apply(terms, inverse):
    rank, cols = terms.shape
    return pl.pallas_call(
        right_apply_body,
        out_shape=(jax.ShapeDtypeStruct((2 * rank, cols), BF16), jax.ShapeDtypeStruct((rank, rank), F32)),
        compiler_params=PARAMS,
        name="right_apply",
    )(terms, inverse)


def match_body(img_col, present_ref, row_count_ref, col_count_ref, row_unit_ref, col_unit_ref, match_ref):
    step = pl.program_id(0)
    row_valid = lax.broadcasted_iota(jnp.int32, (KP, 1), 0) < row_count_ref[step]
    for image in range(img_col):
        cell = slice(image * KP, (image + 1) * KP)
        listed = present_ref[step * img_col + image] > 0

        @pl.when(listed)
        def _():
            scores = lax.dot_general(
                row_unit_ref[...], col_unit_ref[cell, :], (((1,), (1,)), ((), ())), preferred_element_type=F32
            )
            expo = jnp.exp(SHARPNESS * scores)
            col_valid = lax.broadcasted_iota(jnp.int32, (1, KP), 1) < col_count_ref[image]
            by_col = jnp.where(col_valid, expo, 0.0)
            by_row = jnp.where(row_valid, expo, 0.0)
            rowsum = jnp.sum(by_col, axis=1, keepdims=True)
            colsum = jnp.sum(by_row, axis=0, keepdims=True)
            both = jnp.where(row_valid, by_col, 0.0)
            match_ref[:, cell] = both * ((0.5 * KP) * lax.rsqrt(rowsum)) * lax.rsqrt(colsum)

        @pl.when(jnp.logical_not(listed))
        def _():
            match_ref[:, cell] = jnp.zeros((KP, KP), F32)


def half_matches(present, row_count, col_count, row_unit, col_unit):
    rows, cols = row_unit.shape[0], col_unit.shape[0]
    smem = pl.BlockSpec(memory_space=pltpu.SMEM)
    return pl.pallas_call(
        functools.partial(match_body, cols // KP),
        grid=(rows // KP,),
        in_specs=[
            smem, smem, smem,
            pl.BlockSpec((KP, row_unit.shape[1]), lambda i: (i, 0)),
            pl.BlockSpec(col_unit.shape, lambda i: (0, 0)),
        ],
        out_specs=pl.BlockSpec((KP, cols), lambda i: (i, 0)),
        out_shape=jax.ShapeDtypeStruct((rows, cols), F32),
        compiler_params=PARAMS,
        name="half_matches",
        cost_estimate=pl.CostEstimate(flops=rows * cols * 256, bytes_accessed=4 * rows * cols, transcendentals=rows * cols),
    )(present, row_count, col_count, row_unit, col_unit)


def finish_body(img_col, match_ref, left_ref, right_ref, mix_ref, assign_ref, dual_ref, first_ref, second_ref):
    rank = mix_ref.shape[0]

    @pl.when(pl.program_id(0) == 0)
    def _():
        mix_high, mix_low = halves(mix_ref[...])
        high, low = right_ref[:rank, :], right_ref[rank:, :]
        first_ref[: 2 * rank, :] = right_ref[...]
        first_ref[2 * rank :, :] = high
        high, low = halves(dot32(mix_high, high) + dot32(mix_low, high) + dot32(mix_high, low))
        second_ref[:rank, :] = high
        second_ref[rank : 2 * rank, :] = low
        second_ref[2 * rank :, :] = high

    left = jnp.concatenate([left_ref[:, :rank], left_ref[...]], axis=1)
    for image in range(img_col):
        cell = slice(image * KP, (image + 1) * KP)
        half_match = match_ref[:, cell]
        lowrank = dot32(left, first_ref[:, cell])
        half_dual = jnp.clip(lowrank + half_match, 0.0, 1.0) - lowrank
        lowrank = dot32(left, second_ref[:, cell])
        solution = jnp.clip(lowrank + (half_match + half_dual), 0.0, 1.0)
        dual_ref[:, cell] = 2.0 * (half_dual + (solution - lowrank))
        assign_ref[:, cell] = solution.astype(BF16)


def finish(half_match, left_pair, right_pair, mix):
    rows, rank = left_pair.shape[0], mix.shape[0]
    cols = right_pair.shape[1]
    return pl.pallas_call(
        functools.partial(finish_body, cols // KP),
        grid=(rows // KP,),
        in_specs=[
            pl.BlockSpec((KP, cols), lambda i: (i, 0)),
            pl.BlockSpec((KP, 2 * rank), lambda i: (i, 0)),
            pl.BlockSpec((2 * rank, cols), lambda i: (0, 0)),
            pl.BlockSpec((rank, rank), lambda i: (0, 0)),
        ],
        out_specs=(pl.BlockSpec((KP, cols), lambda i: (i, 0)), pl.BlockSpec((KP, cols), lambda i: (i, 0))),
        out_shape=(jax.ShapeDtypeStruct((rows, cols), BF16), jax.ShapeDtypeStruct((rows, cols), F32)),
        scratch_shapes=[pltpu.VMEM((3 * rank, cols), BF16)] * 2,
        compiler_params=PARAMS,
        name="finish",
        cost_estimate=pl.CostEstimate(flops=12 * rows * cols * rank, bytes_accessed=10 * rows * cols, transcendentals=0),
    )(half_match, left_pair, right_pair, mix)


MESH = pl.DeviceIdType.MESH


def greet(peers):
    barrier = pltpu.get_barrier_semaphore()
    for peer in peers:
        pl.semaphore_signal(barrier, inc=1, device_id=peer, device_id_type=MESH)
    pl.semaphore_wait(barrier, len(peers))


def ring_place(place, step, total):
    return lax.rem(place + step, total)


def gram_scratch(row_total, col_total, piece, n):
    dma = pltpu.SemaphoreType.DMA
    return [
        pltpu.VMEM((col_total - 1, piece + 8, n), F32),
        pltpu.VMEM((row_total, piece, n), F32),
        pltpu.VMEM((col_total, piece, n), F32),
        dma((col_total - 1,)), dma((col_total - 1,)),
        dma((row_total - 1,)), dma((row_total - 1,)),
        dma((col_total - 1,)), dma((col_total - 1,)),
    ]


class GramSum:
    def __init__(self, over_rows, row_total, col_total, part_ref, out_ref, extra_ref, scratch):
        self.part_ref, self.out_ref, self.extra_ref = part_ref, out_ref, extra_ref
        (self.col_in, self.row_in, self.spread, self.send_col, self.recv_col,
         self.send_row, self.recv_row, self.send_out, self.recv_out) = scratch
        self.row, self.col = lax.axis_index("row"), lax.axis_index("col")
        self.cols = [(self.row, ring_place(self.col, k, col_total)) for k in range(1, col_total)]
        self.rows = (
            [(ring_place(self.row, k, row_total), self.col) for k in range(1, row_total)] if over_rows else []
        )

    def send(self, source, target, send_sem, recv_sem, peer):
        copy = pltpu.make_async_remote_copy(
            src_ref=source, dst_ref=target, send_sem=send_sem, recv_sem=recv_sem,
            device_id=peer, device_id_type=MESH,
        )
        copy.start()
        return copy

    def begin(self):
        self.first = [
            self.send(self.part_ref.at[peer[1]], self.col_in.at[k], self.send_col.at[k], self.recv_col.at[k], peer)
            for k, peer in enumerate(self.cols)
        ]

    def add_cols(self):
        piece = self.spread.shape[1]
        total = self.part_ref[self.col]
        for k, copy in enumerate(self.first):
            copy.wait_recv()
            total = total + self.col_in[k]
        self.extra_ref[...] = total[piece:, :]
        self.row_in[self.row] = total[:piece, :]
        mine = self.row_in.at[self.row]
        self.second = [
            self.send(mine, mine, self.send_row.at[k], self.recv_row.at[k], peer) for k, peer in enumerate(self.rows)
        ]

    def add_rows(self):
        for copy in self.second:
            copy.wait_recv()
        if self.rows:
            total = self.row_in[0]
            for k in range(1, len(self.rows) + 1):
                total = total + self.row_in[k]
        else:
            total = self.row_in[self.row]
        self.spread[self.col] = total
        mine = self.spread.at[self.col]
        self.third = [
            self.send(mine, mine, self.send_out.at[k], self.recv_out.at[k], peer) for k, peer in enumerate(self.cols)
        ]

    def end(self):
        for copy in self.third:
            copy.wait_recv()
        self.out_ref[...] = self.spread[...]
        for copy in self.first + self.second + self.third:
            copy.wait_send()


def sum_body(over_rows, row_total, col_total, part_ref, out_ref, extra_ref, *scratch):
    gram = GramSum(over_rows, row_total, col_total, part_ref, out_ref, extra_ref, scratch)
    greet(gram.cols + gram.rows)
    gram.begin()
    gram.add_cols()
    gram.add_rows()
    gram.end()


def gram_shapes(gram, extra):
    n = gram.shape[0]
    row_total, col_total = lax.axis_size("row"), lax.axis_size("col")
    piece = n // col_total
    stacked = jnp.concatenate([gram.reshape(col_total, piece, n), extra], axis=1)
    shapes = (jax.ShapeDtypeStruct((col_total, piece, n), F32), jax.ShapeDtypeStruct((8, n), F32))
    return stacked, shapes, gram_scratch(row_total, col_total, piece, n)


def remote_params(call_id):
    return pltpu.CompilerParams(vmem_limit_bytes=48 * 1024 * 1024, collective_id=call_id, has_side_effects=True)


def in_vmem(count):
    return (pl.BlockSpec(memory_space=pltpu.VMEM),) * count


def sum_everywhere(gram, extra, call_id, name):
    n = gram.shape[0]
    stacked, shapes, scratch = gram_shapes(gram, extra)
    total, _ = pl.pallas_call(
        functools.partial(sum_body, True, lax.axis_size("row"), lax.axis_size("col")),
        in_specs=in_vmem(1),
        out_specs=in_vmem(2),
        out_shape=shapes,
        scratch_shapes=scratch,
        compiler_params=remote_params(call_id),
        name=name,
        cost_estimate=pl.CostEstimate(flops=n * n * 10, bytes_accessed=40 * n * n, transcendentals=0),
    )(stacked)
    return total.reshape(n, n)


def chip_peers(col_total):
    row, col = lax.axis_index("row"), lax.axis_index("col")
    core = lax.rem(col, 2)
    chips = col_total // 2
    chip = col // 2
    sibling = (row, col + 1 - 2 * core)
    ahead = [(row, 2 * ring_place(chip, k, chips) + core) for k in range(1, chips)]
    return row, col, core, chip, chips, sibling, ahead


def reduce_body(row_total, col_total, terms_ref, part_ref, out_ref, total_ref, extra_ref, from_core, joined, from_chip, send_core, recv_core, send_chip, recv_chip, *scratch):
    row, col, core, chip, chips, sibling, ahead = chip_peers(col_total)
    gram = GramSum(False, row_total, col_total, part_ref, total_ref, extra_ref, scratch)
    greet(gram.cols)
    gram.begin()
    order = list(range(1, chips)) + [0]
    near, far = {}, {}
    for k in order:
        copy = pltpu.make_async_remote_copy(
            src_ref=terms_ref.at[2 * ring_place(chip, k, chips) + 1 - core], dst_ref=from_core.at[k],
            send_sem=send_core.at[k], recv_sem=recv_core.at[k], device_id=sibling, device_id_type=MESH,
        )
        copy.start()
        near[k] = copy
    for k in order[:-1]:
        near[k].wait_recv()
        joined[k - 1] = terms_ref[2 * ring_place(chip, k, chips) + core] + from_core[k]
        copy = pltpu.make_async_remote_copy(
            src_ref=joined.at[k - 1], dst_ref=from_chip.at[k - 1],
            send_sem=send_chip.at[k - 1], recv_sem=recv_chip.at[k - 1],
            device_id=ahead[k - 1], device_id_type=MESH,
        )
        copy.start()
        far[k] = copy
    gram.add_cols()
    gram.add_rows()
    near[0].wait_recv()
    total = terms_ref[col] + from_core[0]
    for k in order[:-1]:
        far[k].wait_recv()
        total = total + from_chip[k - 1]
    out_ref[...] = total
    gram.end()
    for copy in list(near.values()) + list(far.values()):
        copy.wait_send()


def reduce_over_col(terms, gram, extra, call_id):
    rows, rank = terms.shape
    col_total = lax.axis_size("col")
    chips = col_total // 2
    piece = rows // col_total
    dma = pltpu.SemaphoreType.DMA
    stacked, shapes, scratch = gram_shapes(gram, extra)
    left, total, rest = pl.pallas_call(
        functools.partial(reduce_body, lax.axis_size("row"), col_total),
        in_specs=in_vmem(2),
        out_specs=in_vmem(3),
        out_shape=(jax.ShapeDtypeStruct((piece, rank), F32),) + shapes,
        scratch_shapes=[
            pltpu.VMEM((chips, piece, rank), F32),
            pltpu.VMEM((chips - 1, piece, rank), F32),
            pltpu.VMEM((chips - 1, piece, rank), F32),
            dma((chips,)), dma((chips,)), dma((chips - 1,)), dma((chips - 1,)),
        ] + scratch,
        compiler_params=remote_params(call_id),
        name="left_reduce",
        cost_estimate=pl.CostEstimate(flops=rows * rank, bytes_accessed=40 * rows * rank, transcendentals=0),
    )(terms.reshape(col_total, piece, rank), stacked)
    return left, total.reshape(gram.shape), rest


def gather_body(
    row_total, col_total, piece_ref, part_ref, out_ref, total_ref, extra_ref,
    held, send_core, recv_core, send_chip, recv_chip, *scratch,
):
    row, col, core, chip, chips, sibling, ahead = chip_peers(col_total)
    gram = GramSum(True, row_total, col_total, part_ref, total_ref, extra_ref, scratch)
    held[col] = piece_ref[...]
    greet(gram.cols + gram.rows)
    gram.begin()

    def send(slot, target, send_sem, recv_sem):
        copy = pltpu.make_async_remote_copy(
            src_ref=held.at[slot], dst_ref=held.at[slot], send_sem=send_sem, recv_sem=recv_sem,
            device_id=target, device_id_type=MESH,
        )
        copy.start()
        return copy

    far = [send(col, ahead[k - 1], send_chip.at[k - 1], recv_chip.at[k - 1]) for k in range(1, chips)]
    near = [send(col, sibling, send_core.at[0], recv_core.at[0])]
    gram.add_cols()
    for k in range(1, chips):
        if k == chips - 1:
            gram.add_rows()
        far[k - 1].wait_recv()
        source = 2 * ring_place(chip, chips - k, chips) + core
        near.append(send(source, sibling, send_core.at[k], recv_core.at[k]))
    for copy in near:
        copy.wait_recv()
    out_ref[...] = held[...]
    gram.end()
    for copy in near + far:
        copy.wait_send()


def gather_over_col(piece, gram, extra, call_id):
    rows, width = piece.shape
    col_total = lax.axis_size("col")
    chips = col_total // 2
    dma = pltpu.SemaphoreType.DMA
    stacked, shapes, scratch = gram_shapes(gram, extra)
    whole, total, _ = pl.pallas_call(
        functools.partial(gather_body, lax.axis_size("row"), col_total),
        in_specs=in_vmem(2),
        out_specs=in_vmem(3),
        out_shape=(jax.ShapeDtypeStruct((col_total, rows, width), piece.dtype),) + shapes,
        scratch_shapes=[
            pltpu.VMEM((col_total, rows, width), piece.dtype),
            dma((chips,)), dma((chips,)), dma((chips - 1,)), dma((chips - 1,)),
        ] + scratch,
        compiler_params=remote_params(call_id),
        name="left_gather",
        cost_estimate=pl.CostEstimate(flops=rows, bytes_accessed=80 * rows * width, transcendentals=0),
    )(piece, stacked)
    return whole.reshape(col_total * rows, width), total.reshape(gram.shape)


def own_columns(unit, cols):
    rows = unit.shape[0]
    row_total, col_total = lax.axis_size("row"), lax.axis_size("col")
    start = lax.axis_index("col") * cols
    held = lax.dynamic_slice_in_dim(unit, lax.rem(start, rows), cols, 0)
    found = jnp.where(start // rows == lax.axis_index("row"), held, jnp.zeros_like(held))
    for k in range(1, row_total):
        pairs = []
        for place in range(col_total):
            owner = place * cols // rows
            pairs.append((owner * col_total + place, (owner + k) % row_total * col_total + place))
        found = found + lax.ppermute(held, ("row", "col"), pairs)
    return found


def local(descriptors, image_counts, pair_list, warm_start, factor_init):
    row_place = lax.axis_index("row")
    col_place = lax.axis_index("col")
    rows, cols = warm_start.shape
    img_row, img_col = rows // KP, cols // KP

    row_total, col_total = lax.axis_size("row"), lax.axis_size("col")
    rank = factor_init.shape[1]

    cells = img_row * img_col
    codes = (pair_list[:, 0] - img_row * row_place) * img_col + lax.rem(pair_list[:, 1], img_col)
    hits = (pair_list[:, 1] // img_col)[:, None] == jnp.arange(col_total, dtype=jnp.int32)[None, :]
    marks = codes[:, None] == jnp.arange(cells, dtype=jnp.int32)[None, :]
    flags = jnp.any(hits[:, :, None] & marks[:, None, :], axis=0).astype(F32)
    flags = jnp.pad(flags[:, None, :], ((0, 0), (0, 7), (0, rank - cells)))
    blank = jnp.zeros((col_total, 8, rank), F32)

    wide = descriptors.astype(F32)
    unit = (
        wide * lax.rsqrt(descriptors.shape[1] * (jnp.mean(wide * wide, axis=1, keepdims=True) + EPSILON))
    ).astype(BF16)
    col_unit = own_columns(unit, cols)
    row_count = lax.dynamic_slice_in_dim(image_counts, row_place * img_row, img_row, 0)
    col_count = lax.dynamic_slice_in_dim(image_counts, col_place * img_col, img_col, 0)

    left_terms = left_sum(warm_start, factor_init)
    gram_right = lax.dot_general(factor_init, factor_init, (((0,), (0,)), ((), ())), precision=EXACT)
    left_terms, gram_right, col_unit = lax.optimization_barrier((left_terms, gram_right, col_unit))
    left_terms, gram_right, listed = reduce_over_col(left_terms, gram_right, flags, 1)
    present = (listed[0, :cells] > 0.5).astype(jnp.int32)

    left_pair, gram_left = left_apply(left_terms, ridge_inverse(gram_right))
    left_pair, gram_left = gather_over_col(left_pair, gram_left, blank, 2)
    right_terms = right_sum(left_pair, warm_start)
    gram_late, right_terms, col_unit = lax.optimization_barrier((gram_left, right_terms, col_unit))
    right_terms = lax.psum_scatter(right_terms, "row", scatter_dimension=1, tiled=True)
    half_match = half_matches(present, row_count, col_count, unit, col_unit)
    inverse = ridge_inverse(gram_late)
    right_terms, inverse, half_match = lax.optimization_barrier((right_terms, inverse, half_match))
    right_pair, gram_right = right_apply(right_terms, inverse)
    right_pair = lax.all_gather(right_pair, "row", axis=1, tiled=True)
    gram_right = sum_everywhere(gram_right, blank, 3, "right_gram")
    mix = second_mix(gram_right, gram_left)
    return finish(half_match, left_pair, right_pair, mix)


def solution(mesh):
    return jax.shard_map(
        local,
        mesh=mesh,
        in_specs=(P("row", None), P(), P(("row", "col"), None), P("row", "col"), P("col", None)),
        out_specs=(P("row", "col"), P("row", "col")),
        check_vma=False,
    )
```

```python
import functools

import jax
import jax.numpy as jnp
from jax import lax
from jax.experimental import pallas as pl
from jax.experimental.pallas import tpu as pltpu
from jax.sharding import PartitionSpec as P

KP = 256

EPSILON = 1e-06
SHARPNESS = 10.0
RIDGE = 16.0
EXACT = lax.Precision.HIGHEST
F32 = jnp.float32
BF16 = jnp.bfloat16
PARAMS = pltpu.CompilerParams(vmem_limit_bytes=48 * 1024 * 1024)
SETTLED = 2e-4
ROUGH_TOP = 1000.0 * RIDGE


def halves(x):
    high = x.astype(BF16)
    return high, (x - high.astype(F32)).astype(BF16)


def dot32(a, b):
    return jnp.dot(a, b, preferred_element_type=F32)


def exact(a, b):
    return jnp.dot(a, b, precision=EXACT, preferred_element_type=F32)


def rough_product(a, b):
    a_high, a_low = halves(a)
    b_high, b_low = halves(b)
    return dot32(a_high, b_high) + dot32(a_high, b_low) + dot32(a_low, b_high)


def eye(n):
    return (
        lax.broadcasted_iota(jnp.int32, (n, n), 0) == lax.broadcasted_iota(jnp.int32, (n, n), 1)
    ).astype(F32)


def invert(matrix_ref, inverse_ref):
    n = matrix_ref.shape[0]
    size = jnp.abs(matrix_ref[...])
    top = jnp.max(jnp.sum(size, axis=1, keepdims=True))
    top = jnp.minimum(top, 1.0001 * jnp.sqrt(jnp.sum(jnp.sum(size * size, axis=1, keepdims=True))))
    top = jnp.maximum(top, 1.0001 * RIDGE)
    inverse_ref[...] = (2.0 / (RIDGE + top)) * eye(n)

    def step(product, spread):
        scale = 2.0 / (2.0 - spread * spread)
        rest = (2.0 * scale) * eye(n) - scale * product(matrix_ref[...], inverse_ref[...])
        inverse_ref[...] = product(inverse_ref[...], rest)
        return spread * spread / (2.0 - spread * spread)

    spread = (top - RIDGE) / (top + RIDGE)
    rough = jnp.where(top < ROUGH_TOP, 0.3, 2.0)
    spread = lax.while_loop(lambda s: s > rough, functools.partial(step, rough_product), spread)
    spread = lax.while_loop(lambda s: s > SETTLED, functools.partial(step, exact), spread)
    step(exact, spread)


def inverse_body(gram_ref, out_ref, matrix_ref):
    matrix_ref[...] = gram_ref[...] + RIDGE * eye(gram_ref.shape[0])
    invert(matrix_ref, out_ref)


def ridge_inverse(gram):
    return pl.pallas_call(
        inverse_body,
        out_shape=jax.ShapeDtypeStruct(gram.shape, F32),
        scratch_shapes=[pltpu.VMEM(gram.shape, F32)],
        compiler_params=PARAMS,
        name="ridge_inverse",
        cost_estimate=pl.CostEstimate(flops=200 * gram.shape[0] ** 3, bytes_accessed=8 * gram.size, transcendentals=0),
    )(gram)


def second_body(gram_right_ref, gram_left_ref, out_ref, matrix_ref, inverse_ref, filter_ref):
    n = out_ref.shape[0]
    matrix_ref[...] = gram_right_ref[...] + RIDGE * eye(n)
    invert(matrix_ref, inverse_ref)
    filter_ref[...] = eye(n) - RIDGE * inverse_ref[...]
    out_ref[...] = exact(filter_ref[...], gram_left_ref[...])
    matrix_ref[...] = exact(out_ref[...], filter_ref[...]) + RIDGE * eye(n)
    invert(matrix_ref, inverse_ref)
    out_ref[...] = exact(exact(filter_ref[...], inverse_ref[...]), out_ref[...])


def second_mix(gram_right, gram_left):
    n = gram_right.shape[0]
    return pl.pallas_call(
        second_body,
        out_shape=jax.ShapeDtypeStruct((n, n), F32),
        scratch_shapes=[pltpu.VMEM((n, n), F32)] * 3,
        compiler_params=PARAMS,
        name="second_mix",
        cost_estimate=pl.CostEstimate(flops=400 * n**3, bytes_accessed=12 * n * n, transcendentals=0),
    )(gram_right, gram_left)


def left_sum_body(warm_ref, right_ref, out_ref, high_ref, low_ref):
    @pl.when(pl.program_id(0) == 0)
    def _():
        high_ref[...], low_ref[...] = halves(right_ref[...])

    out_ref[...] = dot32(warm_ref[...], high_ref[...]) + dot32(warm_ref[...], low_ref[...])


def left_sum(warm, right):
    rows, cols = warm.shape
    rank = right.shape[1]
    return pl.pallas_call(
        left_sum_body,
        grid=(rows // KP,),
        in_specs=[
            pl.BlockSpec((KP, cols), lambda i: (i, 0)),
            pl.BlockSpec((cols, rank), lambda i: (0, 0)),
        ],
        out_specs=pl.BlockSpec((KP, rank), lambda i: (i, 0)),
        out_shape=jax.ShapeDtypeStruct((rows, rank), F32),
        scratch_shapes=[pltpu.VMEM((cols, rank), BF16)] * 2,
        compiler_params=PARAMS,
        name="left_sum",
        cost_estimate=pl.CostEstimate(flops=4 * rows * cols * rank, bytes_accessed=2 * rows * cols, transcendentals=0),
    )(warm, right)


def right_sum_body(left_ref, warm_ref, out_ref, gram_ref, turned_ref):
    rank = out_ref.shape[0]

    @pl.when(pl.program_id(0) == 0)
    def _():
        turned_ref[...] = left_ref[...].T
        gram = dot32(turned_ref[...], left_ref[...])
        gram_ref[...] = (gram[:rank, :rank] + gram[rank:, rank:]) + (gram[:rank, rank:] + gram[rank:, :rank])

    out_ref[...] = dot32(turned_ref[:rank, :], warm_ref[...]) + dot32(turned_ref[rank:, :], warm_ref[...])


def right_sum(left_pair, warm):
    rows, cols = warm.shape
    rank = left_pair.shape[1] // 2
    return pl.pallas_call(
        right_sum_body,
        grid=(cols // KP,),
        in_specs=[
            pl.BlockSpec((rows, 2 * rank), lambda i: (0, 0)),
            pl.BlockSpec((rows, KP), lambda i: (0, i)),
        ],
        out_specs=(pl.BlockSpec((rank, KP), lambda i: (0, i)), pl.BlockSpec((rank, rank), lambda i: (0, 0))),
        out_shape=(jax.ShapeDtypeStruct((rank, cols), F32), jax.ShapeDtypeStruct((rank, rank), F32)),
        scratch_shapes=[pltpu.VMEM((2 * rank, rows), BF16)],
        compiler_params=PARAMS,
        name="right_sum",
        cost_estimate=pl.CostEstimate(flops=4 * rows * cols * rank, bytes_accessed=2 * rows * cols, transcendentals=0),
    )(left_pair, warm)


def left_apply_body(terms_ref, inverse_ref, pair_ref):
    rank = terms_ref.shape[1]
    left = exact(terms_ref[...], inverse_ref[...])
    high, low = halves(left)
    pair_ref[:, :rank] = high
    pair_ref[:, rank:] = low


def left_apply(terms, inverse):
    rows, rank = terms.shape
    return pl.pallas_call(
        left_apply_body,
        out_shape=jax.ShapeDtypeStruct((rows, 2 * rank), BF16),
        compiler_params=PARAMS,
        name="left_apply",
    )(terms, inverse)


def right_apply_body(terms_ref, inverse_ref, pair_ref, gram_ref):
    rank = terms_ref.shape[0]
    right = exact(inverse_ref[...], terms_ref[...])
    high, low = halves(right)
    pair_ref[:rank, :] = high
    pair_ref[rank:, :] = low
    gram_ref[...] = exact(right, right.T)


def right_apply(terms, inverse):
    rank, cols = terms.shape
    return pl.pallas_call(
        right_apply_body,
        out_shape=(jax.ShapeDtypeStruct((2 * rank, cols), BF16), jax.ShapeDtypeStruct((rank, rank), F32)),
        compiler_params=PARAMS,
        name="right_apply",
    )(terms, inverse)


def match_body(img_col, present_ref, row_count_ref, col_count_ref, row_unit_ref, col_unit_ref, match_ref):
    step = pl.program_id(0)
    row_valid = lax.broadcasted_iota(jnp.int32, (KP, 1), 0) < row_count_ref[step]
    for image in range(img_col):
        cell = slice(image * KP, (image + 1) * KP)
        listed = present_ref[step * img_col + image] > 0

        @pl.when(listed)
        def _():
            scores = lax.dot_general(
                row_unit_ref[...], col_unit_ref[cell, :], (((1,), (1,)), ((), ())), preferred_element_type=F32
            )
            expo = jnp.exp(SHARPNESS * scores)
            col_valid = lax.broadcasted_iota(jnp.int32, (1, KP), 1) < col_count_ref[image]
            by_col = jnp.where(col_valid, expo, 0.0)
            by_row = jnp.where(row_valid, expo, 0.0)
            rowsum = jnp.sum(by_col, axis=1, keepdims=True)
            colsum = jnp.sum(by_row, axis=0, keepdims=True)
            both = jnp.where(row_valid, by_col, 0.0)
            match_ref[:, cell] = both * ((0.5 * KP) * lax.rsqrt(rowsum)) * lax.rsqrt(colsum)

        @pl.when(jnp.logical_not(listed))
        def _():
            match_ref[:, cell] = jnp.zeros((KP, KP), F32)


def half_matches(present, row_count, col_count, row_unit, col_unit):
    rows, cols = row_unit.shape[0], col_unit.shape[0]
    smem = pl.BlockSpec(memory_space=pltpu.SMEM)
    return pl.pallas_call(
        functools.partial(match_body, cols // KP),
        grid=(rows // KP,),
        in_specs=[
            smem, smem, smem,
            pl.BlockSpec((KP, row_unit.shape[1]), lambda i: (i, 0)),
            pl.BlockSpec(col_unit.shape, lambda i: (0, 0)),
        ],
        out_specs=pl.BlockSpec((KP, cols), lambda i: (i, 0)),
        out_shape=jax.ShapeDtypeStruct((rows, cols), F32),
        compiler_params=PARAMS,
        name="half_matches",
        cost_estimate=pl.CostEstimate(flops=rows * cols * 256, bytes_accessed=4 * rows * cols, transcendentals=rows * cols),
    )(present, row_count, col_count, row_unit, col_unit)


def finish_body(img_col, match_ref, left_ref, right_ref, mix_ref, assign_ref, dual_ref, first_ref, second_ref):
    rank = mix_ref.shape[0]

    @pl.when(pl.program_id(0) == 0)
    def _():
        mix_high, mix_low = halves(mix_ref[...])
        high, low = right_ref[:rank, :], right_ref[rank:, :]
        first_ref[: 2 * rank, :] = right_ref[...]
        first_ref[2 * rank :, :] = high
        high, low = halves(dot32(mix_high, high) + dot32(mix_low, high) + dot32(mix_high, low))
        second_ref[:rank, :] = high
        second_ref[rank : 2 * rank, :] = low
        second_ref[2 * rank :, :] = high

    left = jnp.concatenate([left_ref[:, :rank], left_ref[...]], axis=1)
    for image in range(img_col):
        cell = slice(image * KP, (image + 1) * KP)
        half_match = match_ref[:, cell]
        lowrank = dot32(left, first_ref[:, cell])
        half_dual = jnp.clip(lowrank + half_match, 0.0, 1.0) - lowrank
        lowrank = dot32(left, second_ref[:, cell])
        solution = jnp.clip(lowrank + (half_match + half_dual), 0.0, 1.0)
        dual_ref[:, cell] = 2.0 * (half_dual + (solution - lowrank))
        assign_ref[:, cell] = solution.astype(BF16)


def finish(half_match, left_pair, right_pair, mix):
    rows, rank = left_pair.shape[0], mix.shape[0]
    cols = right_pair.shape[1]
    return pl.pallas_call(
        functools.partial(finish_body, cols // KP),
        grid=(rows // KP,),
        in_specs=[
            pl.BlockSpec((KP, cols), lambda i: (i, 0)),
            pl.BlockSpec((KP, 2 * rank), lambda i: (i, 0)),
            pl.BlockSpec((2 * rank, cols), lambda i: (0, 0)),
            pl.BlockSpec((rank, rank), lambda i: (0, 0)),
        ],
        out_specs=(pl.BlockSpec((KP, cols), lambda i: (i, 0)), pl.BlockSpec((KP, cols), lambda i: (i, 0))),
        out_shape=(jax.ShapeDtypeStruct((rows, cols), BF16), jax.ShapeDtypeStruct((rows, cols), F32)),
        scratch_shapes=[pltpu.VMEM((3 * rank, cols), BF16)] * 2,
        compiler_params=PARAMS,
        name="finish",
        cost_estimate=pl.CostEstimate(flops=12 * rows * cols * rank, bytes_accessed=10 * rows * cols, transcendentals=0),
    )(half_match, left_pair, right_pair, mix)


MESH = pl.DeviceIdType.MESH


def greet(peers):
    barrier = pltpu.get_barrier_semaphore()
    for peer in peers:
        pl.semaphore_signal(barrier, inc=1, device_id=peer, device_id_type=MESH)
    pl.semaphore_wait(barrier, len(peers))


def ring_place(place, step, total):
    return lax.rem(place + step, total)


def gram_scratch(row_total, col_total, piece, n):
    dma = pltpu.SemaphoreType.DMA
    return [
        pltpu.VMEM((col_total - 1, piece + 8, n), F32),
        pltpu.VMEM((row_total, piece, n), F32),
        pltpu.VMEM((col_total, piece, n), F32),
        dma((col_total - 1,)), dma((col_total - 1,)),
        dma((row_total - 1,)), dma((row_total - 1,)),
        dma((col_total - 1,)), dma((col_total - 1,)),
    ]


class GramSum:
    def __init__(self, over_cols, over_rows, row_total, col_total, part_ref, out_ref, extra_ref, scratch):
        self.part_ref, self.out_ref, self.extra_ref = part_ref, out_ref, extra_ref
        (self.col_in, self.row_in, self.spread, self.send_col, self.recv_col,
         self.send_row, self.recv_row, self.send_out, self.recv_out) = scratch
        self.over_cols = over_cols
        self.row, self.col = lax.axis_index("row"), lax.axis_index("col")
        self.cols = [(self.row, ring_place(self.col, k, col_total)) for k in range(1, col_total)]
        self.rows = (
            [(ring_place(self.row, k, row_total), self.col) for k in range(1, row_total)] if over_rows else []
        )

    def send(self, source, target, send_sem, recv_sem, peer):
        copy = pltpu.make_async_remote_copy(
            src_ref=source, dst_ref=target, send_sem=send_sem, recv_sem=recv_sem,
            device_id=peer, device_id_type=MESH,
        )
        copy.start()
        return copy

    def begin(self):
        self.first = [
            self.send(self.part_ref.at[peer[1]], self.col_in.at[k], self.send_col.at[k], self.recv_col.at[k], peer)
            for k, peer in enumerate(self.cols if self.over_cols else [])
        ]

    def add_cols(self):
        piece = self.spread.shape[1]
        total = self.part_ref[self.col]
        for k, copy in enumerate(self.first):
            copy.wait_recv()
            total = total + self.col_in[k]
        self.extra_ref[...] = total[piece:, :]
        self.row_in[self.row] = total[:piece, :]
        mine = self.row_in.at[self.row]
        self.second = [
            self.send(mine, mine, self.send_row.at[k], self.recv_row.at[k], peer) for k, peer in enumerate(self.rows)
        ]

    def add_rows(self):
        for copy in self.second:
            copy.wait_recv()
        if self.rows:
            total = self.row_in[0]
            for k in range(1, len(self.rows) + 1):
                total = total + self.row_in[k]
        else:
            total = self.row_in[self.row]
        self.spread[self.col] = total
        mine = self.spread.at[self.col]
        self.third = [
            self.send(mine, mine, self.send_out.at[k], self.recv_out.at[k], peer) for k, peer in enumerate(self.cols)
        ]

    def end(self):
        for copy in self.third:
            copy.wait_recv()
        self.out_ref[...] = self.spread[...]
        for copy in self.first + self.second + self.third:
            copy.wait_send()


def sum_body(over_cols, row_total, col_total, part_ref, out_ref, extra_ref, *scratch):
    gram = GramSum(over_cols, True, row_total, col_total, part_ref, out_ref, extra_ref, scratch)
    greet(gram.cols + gram.rows)
    gram.begin()
    gram.add_cols()
    gram.add_rows()
    gram.end()


def gram_shapes(gram, extra):
    n = gram.shape[0]
    row_total, col_total = lax.axis_size("row"), lax.axis_size("col")
    piece = n // col_total
    stacked = jnp.concatenate([gram.reshape(col_total, piece, n), extra], axis=1)
    shapes = (jax.ShapeDtypeStruct((col_total, piece, n), F32), jax.ShapeDtypeStruct((8, n), F32))
    return stacked, shapes, gram_scratch(row_total, col_total, piece, n)


def remote_params(call_id):
    return pltpu.CompilerParams(vmem_limit_bytes=48 * 1024 * 1024, collective_id=call_id, has_side_effects=True)


def in_vmem(count):
    return (pl.BlockSpec(memory_space=pltpu.VMEM),) * count


def sum_everywhere(gram, extra, over_cols, call_id, name):
    n = gram.shape[0]
    stacked, shapes, scratch = gram_shapes(gram, extra)
    total, _ = pl.pallas_call(
        functools.partial(sum_body, over_cols, lax.axis_size("row"), lax.axis_size("col")),
        in_specs=in_vmem(1),
        out_specs=in_vmem(2),
        out_shape=shapes,
        scratch_shapes=scratch,
        compiler_params=remote_params(call_id),
        name=name,
        cost_estimate=pl.CostEstimate(flops=n * n * 10, bytes_accessed=40 * n * n, transcendentals=0),
    )(stacked)
    return total.reshape(n, n)


def chip_peers(col_total):
    row, col = lax.axis_index("row"), lax.axis_index("col")
    core = lax.rem(col, 2)
    chips = col_total // 2
    chip = col // 2
    sibling = (row, col + 1 - 2 * core)
    ahead = [(row, 2 * ring_place(chip, k, chips) + core) for k in range(1, chips)]
    return row, col, core, chip, chips, sibling, ahead


def reduce_body(row_total, col_total, terms_ref, part_ref, out_ref, total_ref, extra_ref, from_core, joined, from_chip, send_core, recv_core, send_chip, recv_chip, *scratch):
    row, col, core, chip, chips, sibling, ahead = chip_peers(col_total)
    gram = GramSum(True, False, row_total, col_total, part_ref, total_ref, extra_ref, scratch)
    greet(gram.cols)
    gram.begin()
    order = list(range(1, chips)) + [0]
    near, far = {}, {}
    for k in order:
        copy = pltpu.make_async_remote_copy(
            src_ref=terms_ref.at[2 * ring_place(chip, k, chips) + 1 - core], dst_ref=from_core.at[k],
            send_sem=send_core.at[k], recv_sem=recv_core.at[k], device_id=sibling, device_id_type=MESH,
        )
        copy.start()
        near[k] = copy
    for k in order[:-1]:
        near[k].wait_recv()
        joined[k - 1] = terms_ref[2 * ring_place(chip, k, chips) + core] + from_core[k]
        copy = pltpu.make_async_remote_copy(
            src_ref=joined.at[k - 1], dst_ref=from_chip.at[k - 1],
            send_sem=send_chip.at[k - 1], recv_sem=recv_chip.at[k - 1],
            device_id=ahead[k - 1], device_id_type=MESH,
        )
        copy.start()
        far[k] = copy
    gram.add_cols()
    gram.add_rows()
    near[0].wait_recv()
    total = terms_ref[col] + from_core[0]
    for k in order[:-1]:
        far[k].wait_recv()
        total = total + from_chip[k - 1]
    out_ref[...] = total
    gram.end()
    for copy in list(near.values()) + list(far.values()):
        copy.wait_send()


def reduce_over_col(terms, gram, extra, call_id):
    rows, rank = terms.shape
    col_total = lax.axis_size("col")
    chips = col_total // 2
    piece = rows // col_total
    dma = pltpu.SemaphoreType.DMA
    stacked, shapes, scratch = gram_shapes(gram, extra)
    left, total, rest = pl.pallas_call(
        functools.partial(reduce_body, lax.axis_size("row"), col_total),
        in_specs=in_vmem(2),
        out_specs=in_vmem(3),
        out_shape=(jax.ShapeDtypeStruct((piece, rank), F32),) + shapes,
        scratch_shapes=[
            pltpu.VMEM((chips, piece, rank), F32),
            pltpu.VMEM((chips - 1, piece, rank), F32),
            pltpu.VMEM((chips - 1, piece, rank), F32),
            dma((chips,)), dma((chips,)), dma((chips - 1,)), dma((chips - 1,)),
        ] + scratch,
        compiler_params=remote_params(call_id),
        name="left_reduce",
        cost_estimate=pl.CostEstimate(flops=rows * rank, bytes_accessed=40 * rows * rank, transcendentals=0),
    )(terms.reshape(col_total, piece, rank), stacked)
    return left, total.reshape(gram.shape), rest


def gather_body(
    col_total, piece_ref, out_ref, held, send_core, recv_core, send_chip, recv_chip
):
    row, col, core, chip, chips, sibling, ahead = chip_peers(col_total)
    held[col] = piece_ref[...]
    greet([sibling] + ahead)

    def send(slot, target, send_sem, recv_sem):
        copy = pltpu.make_async_remote_copy(
            src_ref=held.at[slot], dst_ref=held.at[slot], send_sem=send_sem, recv_sem=recv_sem,
            device_id=target, device_id_type=MESH,
        )
        copy.start()
        return copy

    far = [send(col, ahead[k - 1], send_chip.at[k - 1], recv_chip.at[k - 1]) for k in range(1, chips)]
    near = [send(col, sibling, send_core.at[0], recv_core.at[0])]
    for k in range(1, chips):
        far[k - 1].wait_recv()
        source = 2 * ring_place(chip, chips - k, chips) + core
        near.append(send(source, sibling, send_core.at[k], recv_core.at[k]))
    for copy in near:
        copy.wait_recv()
    out_ref[...] = held[...]
    for copy in near + far:
        copy.wait_send()


def gather_over_col(piece, call_id):
    rows, width = piece.shape
    col_total = lax.axis_size("col")
    chips = col_total // 2
    dma = pltpu.SemaphoreType.DMA
    whole = pl.pallas_call(
        functools.partial(gather_body, col_total),
        in_specs=in_vmem(1),
        out_specs=pl.BlockSpec(memory_space=pltpu.VMEM),
        out_shape=jax.ShapeDtypeStruct((col_total, rows, width), piece.dtype),
        scratch_shapes=[
            pltpu.VMEM((col_total, rows, width), piece.dtype),
            dma((chips,)), dma((chips,)), dma((chips - 1,)), dma((chips - 1,)),
        ],
        compiler_params=remote_params(call_id),
        name="left_gather",
        cost_estimate=pl.CostEstimate(flops=rows, bytes_accessed=80 * rows * width, transcendentals=0),
    )(piece)
    return whole.reshape(col_total * rows, width)


def own_columns(unit, cols):
    rows = unit.shape[0]
    row_total, col_total = lax.axis_size("row"), lax.axis_size("col")
    start = lax.axis_index("col") * cols
    held = lax.dynamic_slice_in_dim(unit, lax.rem(start, rows), cols, 0)
    found = jnp.where(start // rows == lax.axis_index("row"), held, jnp.zeros_like(held))
    for k in range(1, row_total):
        pairs = []
        for place in range(col_total):
            owner = place * cols // rows
            pairs.append((owner * col_total + place, (owner + k) % row_total * col_total + place))
        found = found + lax.ppermute(held, ("row", "col"), pairs)
    return found


def local(descriptors, image_counts, pair_list, warm_start, factor_init):
    row_place = lax.axis_index("row")
    col_place = lax.axis_index("col")
    rows, cols = warm_start.shape
    img_row, img_col = rows // KP, cols // KP

    row_total, col_total = lax.axis_size("row"), lax.axis_size("col")
    rank = factor_init.shape[1]

    cells = img_row * img_col
    codes = (pair_list[:, 0] - img_row * row_place) * img_col + lax.rem(pair_list[:, 1], img_col)
    hits = (pair_list[:, 1] // img_col)[:, None] == jnp.arange(col_total, dtype=jnp.int32)[None, :]
    marks = codes[:, None] == jnp.arange(cells, dtype=jnp.int32)[None, :]
    flags = jnp.any(hits[:, :, None] & marks[:, None, :], axis=0).astype(F32)
    flags = jnp.pad(flags[:, None, :], ((0, 0), (0, 7), (0, rank - cells)))
    blank = jnp.zeros((col_total, 8, rank), F32)

    wide = descriptors.astype(F32)
    unit = (
        wide * lax.rsqrt(descriptors.shape[1] * (jnp.mean(wide * wide, axis=1, keepdims=True) + EPSILON))
    ).astype(BF16)
    col_unit = own_columns(unit, cols)
    row_count = lax.dynamic_slice_in_dim(image_counts, row_place * img_row, img_row, 0)
    col_count = lax.dynamic_slice_in_dim(image_counts, col_place * img_col, img_col, 0)

    left_terms = left_sum(warm_start, factor_init)
    gram_right = lax.dot_general(factor_init, factor_init, (((0,), (0,)), ((), ())), precision=EXACT)
    left_terms, gram_right, col_unit = lax.optimization_barrier((left_terms, gram_right, col_unit))
    left_terms, gram_right, listed = reduce_over_col(left_terms, gram_right, flags, 1)
    present = (listed[0, :cells] > 0.5).astype(jnp.int32)

    left_pair = gather_over_col(left_apply(left_terms, ridge_inverse(gram_right)), 2)
    right_terms, gram_left = right_sum(left_pair, warm_start)
    gram_left, right_terms, col_unit = lax.optimization_barrier((gram_left, right_terms, col_unit))
    right_terms = lax.psum_scatter(right_terms, "row", scatter_dimension=1, tiled=True)
    half_match = half_matches(present, row_count, col_count, unit, col_unit)
    gram_left = sum_everywhere(gram_left, blank, False, 4, "left_gram")
    inverse = ridge_inverse(gram_left)
    right_terms, inverse, half_match = lax.optimization_barrier((right_terms, inverse, half_match))
    right_pair, gram_right = right_apply(right_terms, inverse)
    right_pair = lax.all_gather(right_pair, "row", axis=1, tiled=True)
    gram_right = sum_everywhere(gram_right, blank, True, 3, "right_gram")
    mix = second_mix(gram_right, gram_left)
    return finish(half_match, left_pair, right_pair, mix)


def solution(mesh):
    return jax.shard_map(
        local,
        mesh=mesh,
        in_specs=(P("row", None), P(), P(("row", "col"), None), P("row", "col"), P("col", None)),
        out_specs=(P("row", "col"), P("row", "col")),
        check_vma=False,
    )
```
